256 devices in a mesh: rep: 4 (over y_lo, core), shard: 64 (over z, x, y_hi).
Axes of the slice: x: 4, y: 4 (y_hi: 2, y_lo: 2; y = y_hi * 2 + y_lo), z: 8, core: 2. Of those that a mesh axis runs over, the one named last changes fastest.
Arguments:
- local_weights: bfloat16 [4, 1024, 8192], P('rep', 'shard'), may hold values from -6 to 6
- base: bfloat16 [1024, 8192], P('shard'), may hold values from -6 to 6
- error: float32 [4, 1024, 8192], P('rep', 'shard'), may hold values from -4 to 4
- momentum: float32 [1024, 8192], P('shard'), may hold values from -4 to 4
- signs: int32 [8192], replicated, may hold values from -1 to 1, as said below
- kept: int32 [2, 1024], replicated, may hold values from 0 to 4095, as said below
Outputs:
- new_base: bfloat16 [1024, 8192], replicated
- new_error: float32 [4, 1024, 8192], P('rep', 'shard')
- new_momentum: float32 [1024, 8192], P('shard')
The draws below stay inside these ranges and needn't reach their ends.
Inputs may be any that keep to these rules, and one draw needn't show every extreme that they name: `signs`: each entry is -1 or 1. `kept`: the 1024 positions of each block are distinct.
All inputs are finite; a program needn't handle non-finite values.
Results may differ from the reference program's by a relative error of at most 0.001.
Values may be sent and summed in bfloat16 or wider, within the bound.
A program may use at most 128 MiB of HBM per device.

```python
import jax
import jax.numpy as jnp
from jax import lax

D = 8192
FAC = 64
BLOCK = 4096
NBLK = 2
KEEP = 1024
ROWS = 1024
REPS = 4


def draw_signs(key, part):
    key = jax.random.fold_in(key, 11)
    return (2 * jax.random.randint(key, (D,), 0, 2) - 1).astype(jnp.int32)


def draw_kept(key, part):
    key = jax.random.fold_in(key, 23)
    keys = jax.random.split(key, NBLK)

    def one_block(block_key):
        inner = jax.random.permutation(block_key, BLOCK - 2) + 1
        ends = jnp.array([0, BLOCK - 1], jnp.int32)
        return jnp.concatenate([ends, inner[:KEEP - 2].astype(jnp.int32)])
    return jax.vmap(one_block)(keys).astype(jnp.int32)


def steps_of(own_key, dims, cuts, smallest, top_value):
    factor_of, own = 1.0, jax.random.fold_in(own_key, 6)
    for axis_at, parts in cuts:
        heights = jnp.exp(jax.random.uniform(jax.random.fold_in(own, axis_at), (parts,), jnp.float32, smallest / len(cuts), top_value / len(cuts)))
        factor_of = factor_of * jnp.repeat(heights, dims[axis_at] // parts).reshape([-1 if axis == axis_at else 1 for axis in range(len(dims))])
    return factor_of


def scatter_about(rng, shape, width, most, cuts=(), kind=jnp.bfloat16):
    entries = width * jax.random.normal(rng, shape, jnp.float32)
    if cuts:
        entries = entries * steps_of(rng, shape, cuts, -0.22, 0.18)
    return jnp.clip(entries, -most, most).astype(kind)


def setup_inputs(seed: int = 0) -> dict:
    streams_of = jax.random.split(jax.random.key(seed), 7)
    local_weights = scatter_about(streams_of[0], (REPS, ROWS, D), 1.0, 6.0, ((0, 4), (1, 64)))
    base = scatter_about(streams_of[1], (ROWS, D), 1.0, 6.0, ((0, 64),))
    error = scatter_about(streams_of[2], (REPS, ROWS, D), 0.5, 4.0, ((0, 4), (1, 64)), jnp.float32)
    momentum = scatter_about(streams_of[3], (ROWS, D), 0.5, 4.0, ((0, 64),), jnp.float32)
    signs = draw_signs(jax.random.fold_in(streams_of[6], 71), 0)
    kept = draw_kept(jax.random.fold_in(streams_of[6], 71), 0)
    return {"local_weights": local_weights, "base": base, "error": error, "momentum": momentum, "signs": signs, "kept": kept}


momentum_rate = 0.9
outer_rate = 0.7


def hadamard(order):
    index = jnp.arange(order, dtype=jnp.int32)
    both = jnp.bitwise_and(index[:, None], index[None, :])
    parity = jnp.zeros((order, order), jnp.int32)
    for bit in range(order.bit_length() - 1):
        parity = parity + jnp.bitwise_and(jnp.right_shift(both, bit), 1)
    return (1 - 2 * (parity % 2)).astype(jnp.float32)


def rotate(values, table):
    rows, nblk, block = values.shape
    order = table.shape[0]
    grid = values.reshape(rows, nblk, order, order)
    first = jnp.einsum("rkab,ac->rkcb", grid, table, precision=lax.Precision.HIGHEST)
    second = jnp.einsum("rkcb,bd->rkcd", first, table, precision=lax.Precision.HIGHEST)
    return second.reshape(rows, nblk, block) / order


def reference(local_weights, base, error, momentum, signs, kept):
    table = hadamard(FAC)
    sign_rows = signs.astype(jnp.float32).reshape(NBLK, BLOCK)
    blocks = jnp.arange(NBLK, dtype=jnp.int32)[:, None]
    mask = jnp.zeros((NBLK, BLOCK), jnp.float32).at[blocks, kept].set(1.0)
    base_wide = base.astype(jnp.float32)
    total = jnp.zeros((ROWS, NBLK, KEEP), jnp.float32)
    errors = []
    for rep in range(REPS):
        compensated = base_wide - local_weights[rep].astype(jnp.float32) + error[rep]
        rotated = rotate(compensated.reshape(ROWS, NBLK, BLOCK) * sign_rows, table)
        total = total + rotated[:, blocks, kept]
        dropped = rotate(rotated * (1.0 - mask), table) * sign_rows
        errors.append(dropped.reshape(ROWS, D))
    average = total / REPS
    full = jnp.zeros((ROWS, NBLK, BLOCK), jnp.float32).at[:, blocks, kept].set(average)
    outer = (rotate(full, table) * sign_rows).reshape(ROWS, D)
    new_momentum = momentum_rate * momentum + outer
    new_base = (base_wide - outer_rate * (outer + momentum_rate * new_momentum)).astype(jnp.bfloat16)
    return new_base, jnp.stack(errors), new_momentum
```

```python
import functools
import heapq

import jax
import jax.numpy as jnp
from jax import lax
from jax.experimental import pallas as pl
from jax.experimental.pallas import tpu as pltpu
from jax.sharding import PartitionSpec as P

MESH = pl.DeviceIdType.MESH
SIZES = {"x": 4, "y": 4, "z": 8}
AXES = ("x", "y", "z")
ROWS, QUARTER, LANES = 16, 2048, 128
PARTS = {"A": ("xyz", 0, 5), "B": ("yzx", 5, 6), "C": ("zxy", 11, 5)}
READY = {"A": 0.0, "B": 0.6, "C": 1.2}
TILE_US, HOP_US, OP_US, LEAD_US = 0.089, 1.7, 0.03, 1.0


def ring(axis, tiles):
    half = SIZES[axis] // 2
    middle = tiles // 2
    chains = []
    for sign, first, last in ((1, 0, middle), (-1, middle, tiles)):
        chains.append((sign, [(hop, 0, tiles) for hop in range(1, half)] + [(half, first, last)]))
    return chains


def messages():
    found = {}

    def chain(part, stage, tag, axis, region, tiles, start):
        order, low, _ = PARTS[part]
        arrived = {0: start}
        for sign, hops in ring(axis, tiles):
            before = start
            for hop, first, last in hops:
                name = (part, stage) + tag + (sign, hop)
                place = dict(region)
                place[axis] = -sign * hop
                found[name] = dict(
                    part=part, stage=stage, axis=axis, sign=sign, hop=hop, region=place,
                    tiles=(low + first, low + last), after=list(before),
                )
                before = [name]
                key = -sign * hop if 2 * hop < SIZES[axis] else SIZES[axis] // 2
                arrived.setdefault(key, []).append(name)
        return arrived

    for part, (order, _, tiles) in PARTS.items():
        one, two, three = order
        own = [("own", part)]
        firsts = chain(part, 1, (), one, {one: 0, two: 0, three: 0}, tiles, own)
        seconds = {}
        for off, names in firsts.items():
            got = chain(part, 2, (off,), two, {one: off, two: 0, three: 0}, tiles, names)
            for place, news in got.items():
                if place != 0:
                    seconds.setdefault(place, []).extend(news)
        for off, names in firsts.items():
            chain(part, 3, (off, "one"), three, {one: off, two: 0, three: 0}, tiles, names)
        for off, names in seconds.items():
            chain(part, 3, (off, "all"), three, {one: None, two: off, three: 0}, tiles, names)
    return found


def count(message):
    wide = 1
    for axis, place in message["region"].items():
        wide *= SIZES[axis] if place is None else 1
    return wide * (message["tiles"][1] - message["tiles"][0])


def schedule(found):
    users = {}
    for name, message in found.items():
        for before in message["after"]:
            users.setdefault(before, []).append(name)
    needs = {name: len(message["after"]) for name, message in found.items()}
    events, queues, active, steps = [], {}, {}, []
    ticket = 0

    def push(time, rank, kind, what):
        nonlocal ticket
        ticket += 1
        heapq.heappush(events, (time, rank, ticket, kind, what))

    def kick(link, time):
        if active.get(link) or not queues.get(link):
            return
        _, _, ready, name = heapq.heappop(queues[link])
        active[link] = True
        length = count(found[name]) * TILE_US
        steps.append((max(ready, time - LEAD_US), 1, len(steps), "send", name))
        push(time + length, 1, "free", link)
        push(time + length + HOP_US, 0, "arrive", name)

    for part, time in READY.items():
        push(time, 0, "arrive", ("own", part))
    clock = 0.0
    while events:
        time, _, _, kind, what = heapq.heappop(events)
        if kind == "free":
            active[what] = False
            kick(what, time)
        elif kind == "issue":
            message = found[what]
            link = (message["axis"], message["sign"])
            ticket += 1
            heapq.heappush(queues.setdefault(link, []), (message["stage"], ticket, time, what))
            kick(link, time)
        else:
            clock = max(clock, time) + OP_US
            steps.append((clock, 0, len(steps), "wait", what))
            for name in users.get(what, []):
                needs[name] -= 1
                if needs[name] == 0:
                    clock += OP_US
                    push(clock, 0, "issue", name)
            clock += OP_US
    steps.sort()
    return [(kind, what) for _, _, _, kind, what in steps]


def forwards(found):
    groups = {}
    for name, message in found.items():
        part = message["part"]
        order, low, tiles = PARTS[part]
        one, two, three = order
        fold = lambda axis: None if message["region"][axis] is None else message["region"][axis] % SIZES[axis]
        if message["stage"] == 1:
            key = (part, 1, 0, 0)
        elif message["stage"] == 2:
            key = (part, 2, fold(two), 0)
        else:
            key = (part, 3, fold(two), fold(three))
        region = {one: None, two: key[2], three: key[3]}
        groups.setdefault(key, (region, (low, low + tiles), []))[2].append(name)
    for part in PARTS:
        groups[(part, 1, 0, 0)][2].append(("own", part))
    return list(groups.values())


def parity_table(rows, columns):
    i = lax.broadcasted_iota(jnp.int32, (rows, columns), 0)
    j = lax.broadcasted_iota(jnp.int32, (rows, columns), 1)
    both = jnp.bitwise_and(jnp.bitwise_and(i, j), LANES - 1)
    for shift in (4, 2, 1):
        both = jnp.bitwise_xor(both, jnp.right_shift(both, shift))
    return (1 - 2 * jnp.bitwise_and(both, 1)).astype(jnp.bfloat16)


def rotate(tiles, table):
    number, rows, lanes = tiles.shape
    flat = tiles.reshape(number * rows, lanes)
    high = flat.astype(jnp.bfloat16)
    low = (flat - high.astype(jnp.float32)).astype(jnp.bfloat16)
    flat = jnp.dot(jnp.concatenate([high, low], axis=1), table, preferred_element_type=jnp.float32)
    near = 1
    while near < number:
        pairs = flat.reshape(number // (2 * near), 2, near * rows, lanes)
        flat = jnp.concatenate(
            [(pairs[:, 0] + pairs[:, 1])[:, None], (pairs[:, 0] - pairs[:, 1])[:, None]], axis=1
        )
        near *= 2
    return flat.reshape(number, rows, lanes)


def sketch_kernel(lw_ref, base_ref, error_ref, signs_ref, kept_ref, kept_part_ref, dropped_ref):
    table = parity_table(2 * LANES, LANES)
    nblk, keep = kept_ref.shape
    tiles = signs_ref.shape[0] // nblk
    block = tiles * LANES
    scale = 1.0 / 64.0
    for b in range(nblk):
        columns = pl.ds(b * block, block)
        compensated = (
            base_ref[:, columns].astype(jnp.float32) - lw_ref[0, :, columns].astype(jnp.float32)
        ) + error_ref[0, :, columns]
        comp = jnp.stack([compensated[:, t * LANES:(t + 1) * LANES] for t in range(tiles)])
        signs = signs_ref[pl.ds(b * tiles, tiles), :].astype(jnp.float32)[:, None, :]
        places = kept_ref[pl.ds(b, 1), :]
        outer_hot = lax.broadcasted_iota(jnp.int32, (tiles, keep), 0) == jnp.right_shift(places, 7)
        inner_hot = lax.broadcasted_iota(jnp.int32, (LANES, keep), 0) == jnp.bitwise_and(places, LANES - 1)
        mask = lax.dot_general(
            outer_hot.astype(jnp.bfloat16), inner_hot.astype(jnp.bfloat16),
            (((1,), (1,)), ((), ())), preferred_element_type=jnp.float32,
        )[:, None, :]
        rotated = rotate(comp * signs, table) * scale
        back = rotate(jnp.where(mask > 0.5, rotated, 0.0), table) * (signs * scale)
        rest = comp - back
        half = tiles // 2
        for t in range(tiles):
            kept_part_ref[2 * b + t // half, :, pl.ds((t % half) * LANES, LANES)] = back[t]
            dropped_ref[:, pl.ds(b * block + t * LANES, LANES)] = rest[t]


def exchange_kernel(
    steps, found, joined,
    part_ref, base_ref, momentum_ref, whole_ref, fresh_ref,
    near, far, mine, outer,
    near_send, near_recv, far_send, far_recv, outer_send, outer_recv,
    stage_send, message_recv, core_send, core_recv,
):
    rep, shard = lax.axis_index("rep"), lax.axis_index("shard")
    p, c = rep // 2, rep % 2
    here = {"x": (shard // 2) % 4, "y": (shard % 2) * 2 + p, "z": shard // 8}

    def device(x, y, z, core):
        return ((y % 2) * 2 + core, z * 8 + x * 2 + y // 2)

    def moved(axis, sign):
        there = dict(here)
        there[axis] = lax.rem(here[axis] + sign + SIZES[axis], SIZES[axis])
        return device(there["x"], there["y"], there["z"], c)

    other_core = device(here["x"], here["y"], here["z"], 1 - c)
    partner = device(here["x"], (shard % 2) * 2 + 1 - p, here["z"], c)
    around = {(axis, sign): moved(axis, sign) for axis in AXES for sign in (1, -1)}

    barrier = pltpu.get_barrier_semaphore()
    for target in list(around.values()) + [other_core]:
        pl.semaphore_signal(barrier, inc=1, device_id=target, device_id_type=MESH)
    pl.semaphore_wait(barrier, 7)

    def remote(source, target, send, recv, where):
        return pltpu.make_async_remote_copy(
            src_ref=source, dst_ref=target, send_sem=send, recv_sem=recv, device_id=where, device_id_type=MESH
        )

    def at(region, tiles, core):
        index = {}
        for axis in AXES:
            place = region[axis]
            if place is None:
                index[axis] = None
            else:
                index[axis] = lax.rem(here[axis] + place + SIZES[axis], SIZES[axis])
        y_high = slice(None) if index["y"] is None else index["y"] // 2
        y_low = slice(None) if index["y"] is None else index["y"] % 2
        z = slice(None) if index["z"] is None else index["z"]
        x = slice(None) if index["x"] is None else index["x"]
        return whole_ref.at[z, x, y_high, y_low, core, :, pl.ds(tiles[0] * LANES, (tiles[1] - tiles[0]) * LANES)]

    to_far = remote(part_ref.at[2 * (1 - p) + 1 - c], near.at[0], near_send.at[0], near_recv.at[0], other_core)
    to_mine = remote(part_ref.at[2 * p + 1 - c], near.at[1], near_send.at[1], near_recv.at[1], other_core)
    to_far.start()
    to_mine.start()
    to_far.wait_recv()
    pieces = {}
    for i, (part, (_, low, tiles)) in enumerate(PARTS.items()):
        columns = pl.ds(low * LANES, tiles * LANES)
        mine[:, columns] = part_ref[2 * (1 - p) + c, :, columns] + near[0, :, columns]
        pieces[part] = remote(mine.at[:, columns], far.at[:, columns], far_send.at[i], far_recv.at[i], partner)
        pieces[part].start()
    to_mine.wait_recv()

    names = {name: i for i, name in enumerate(found)}
    sums = {(part, stage): i for i, (part, stage) in enumerate((part, stage) for part in PARTS for stage in (1, 2, 3))}

    def sent(name):
        message = found[name]
        region = dict(message["region"])
        region[message["axis"]] += message["sign"]
        source = at(region, message["tiles"], c)
        return remote(
            source, source, stage_send.at[sums[message["part"], message["stage"]]],
            message_recv.at[names[name]], around[message["axis"], message["sign"]],
        )

    def received(name):
        message = found[name]
        place = at(message["region"], message["tiles"], c)
        return remote(
            place, place, stage_send.at[sums[message["part"], message["stage"]]],
            message_recv.at[names[name]], around[message["axis"], message["sign"]],
        )

    def own(part):
        _, low, tiles = PARTS[part]
        columns = pl.ds(low * LANES, tiles * LANES)
        pieces[part].wait_recv()
        total = (part_ref[2 * p + c, :, columns] + near[1, :, columns]) + far[:, columns]
        step = total * 0.25
        outer[2 * p + c, :, columns] = step
        wide = pl.ds(pl.multiple_of((2 * p + c) * QUARTER + low * LANES, LANES), tiles * LANES)
        fresh = 0.9 * momentum_ref[:, wide] + step
        lowered = base_ref[:, wide].astype(jnp.float32) - 0.7 * (step + 0.9 * fresh)
        whole_ref[here["z"], here["x"], here["y"] // 2, p, c, :, columns] = lowered.astype(jnp.bfloat16)

    waiting = [[set(group), region, tiles] for region, tiles, group in joined]
    to_core = []
    outer_copies = []
    owned = 0
    for kind, what in steps:
        if kind == "send":
            sent(what).start()
            continue
        if what[0] == "own":
            own(what[1])
            owned += 1
            if owned == len(PARTS):
                quarter = outer.at[2 * p + c]
                outer_copies = [
                    remote(quarter, quarter, outer_send.at[0], outer_recv.at[0], partner),
                    remote(quarter, quarter, outer_send.at[1], outer_recv.at[1], other_core),
                ]
                for copy in outer_copies:
                    copy.start()
        else:
            received(what).wait_recv()
        for entry in waiting:
            entry[0].discard(what)
        for entry in [entry for entry in waiting if not entry[0]]:
            waiting.remove(entry)
            place = at(entry[1], entry[2], c)
            remote(place, place, core_send, core_recv, other_core).start()

    their = outer.at[2 * (1 - p) + c]
    remote(their, their, outer_send.at[0], outer_recv.at[0], partner).wait_recv()
    last = remote(their, their, outer_send.at[2], outer_recv.at[2], other_core)
    last.start()
    remote(outer.at[2 * p + 1 - c], outer.at[2 * p + 1 - c], outer_send.at[1], outer_recv.at[1], other_core).wait_recv()
    final = outer.at[2 * (1 - p) + 1 - c]
    remote(final, final, outer_send.at[2], outer_recv.at[2], other_core).wait_recv()
    for q in range(4):
        columns = pl.ds(q * QUARTER, QUARTER)
        fresh_ref[:, columns] = 0.9 * momentum_ref[:, columns] + outer[q]

    everything = whole_ref.at[:, :, :, :, 1 - c]
    remote(everything, everything, core_send, core_recv, other_core).wait_recv()
    everything = whole_ref.at[:, :, :, :, c]
    remote(everything, everything, core_send, core_recv, other_core).wait_send()
    for part, (order, low, tiles) in PARTS.items():
        columns = pl.ds(low * LANES, tiles * LANES)
        for stage in (1, 2, 3):
            ends = {axis: 1 for axis in AXES}
            for axis in order[:stage - 1]:
                ends[axis] = SIZES[axis]
            ends[order[stage - 1]] = SIZES[order[stage - 1]] - 1
            spans = {1: [(1, 1)], 3: [(1, 2), (1, 1)], 4: [(2, 2)]}[ends["y"]]
            for y_high, y_low in spans:
                place = whole_ref.at[
                    pl.ds(0, ends["z"]), pl.ds(0, ends["x"]), pl.ds(0, y_high), pl.ds(0, y_low), c, :, columns
                ]
                remote(
                    place, place, stage_send.at[sums[part, stage]], core_recv, other_core
                ).wait_send()
    to_far.wait_send()
    to_mine.wait_send()
    for copy in list(pieces.values()) + outer_copies + [last]:
        copy.wait_send()


def store_kernel(whole_ref, fresh_ref, dropped_ref, base_out, error_out, momentum_out, sems):
    copies = [
        pltpu.make_async_copy(fresh_ref, momentum_out, sems.at[0]),
        pltpu.make_async_copy(dropped_ref, error_out.at[0], sems.at[1]),
    ]
    for z in range(whole_ref.shape[0]):
        for low in range(2):
            for core in range(2):
                copies.append(pltpu.make_async_copy(
                    whole_ref.at[z, :, :, low, core],
                    base_out.at[z, :, :, :, pl.ds((2 * low + core) * QUARTER, QUARTER)],
                    sems.at[len(copies)],
                ))
    for copy in copies:
        copy.start()
    for copy in copies:
        copy.wait()


def shards(local_weights, base, error, momentum, signs, kept):
    rows, width = base.shape
    vmem = pl.BlockSpec(memory_space=pltpu.VMEM)
    hbm = pl.BlockSpec(memory_space=pl.ANY)
    held = lambda array: pltpu.with_memory_space_constraint(array, pltpu.VMEM)
    part, dropped = pl.pallas_call(
        sketch_kernel,
        out_shape=(pltpu.VMEM((4, rows, QUARTER), jnp.float32), pltpu.VMEM((rows, width), jnp.float32)),
        in_specs=[vmem] * 5,
        out_specs=(vmem, vmem),
        compiler_params=pltpu.CompilerParams(vmem_limit_bytes=24 << 20),
        name="sketch",
    )(local_weights, base, error, signs.reshape(width // LANES, LANES), kept)

    found = messages()
    steps, joined = schedule(found), forwards(found)
    dma = pltpu.SemaphoreType.DMA
    whole, fresh = pl.pallas_call(
        functools.partial(exchange_kernel, steps, found, joined),
        out_shape=(
            pltpu.VMEM((8, 4, 2, 2, 2, rows, QUARTER), jnp.bfloat16),
            pltpu.VMEM((rows, width), jnp.float32),
        ),
        in_specs=[vmem] * 3,
        out_specs=(vmem, vmem),
        scratch_shapes=[
            pltpu.VMEM((2, rows, QUARTER), jnp.float32),
            pltpu.VMEM((rows, QUARTER), jnp.float32),
            pltpu.VMEM((rows, QUARTER), jnp.float32),
            pltpu.VMEM((4, rows, QUARTER), jnp.float32),
            dma((2,)), dma((2,)), dma((3,)), dma((3,)), dma((3,)), dma((3,)),
            dma((9,)), dma((len(found),)), dma, dma,
        ],
        compiler_params=pltpu.CompilerParams(
            collective_id=0, has_side_effects=True, vmem_limit_bytes=16 << 20
        ),
        name="exchange",
    )(held(part), base, momentum)

    new_base, new_error, new_momentum = pl.pallas_call(
        store_kernel,
        out_shape=(
            jax.ShapeDtypeStruct((8, 4, 2, rows, width), jnp.bfloat16),
            jax.ShapeDtypeStruct((1, rows, width), jnp.float32),
            jax.ShapeDtypeStruct((rows, width), jnp.float32),
        ),
        in_specs=[vmem] * 3,
        out_specs=(hbm, hbm, hbm),
        scratch_shapes=[dma((34,))],
        compiler_params=pltpu.CompilerParams(vmem_limit_bytes=16 << 20),
        name="store",
    )(held(whole), held(fresh), held(dropped))
    return (new_base.reshape(64 * rows, width), new_error, new_momentum)


def solution(mesh):
    in_specs = (
        P("rep", "shard", None),
        P("shard", None),
        P("rep", "shard", None),
        P("shard", None),
        P(),
        P(),
    )
    out_specs = (P(), P("rep", "shard", None), P("shard", None))
    return jax.shard_map(shards, mesh=mesh, in_specs=in_specs, out_specs=out_specs, check_vma=False)
```

```python
import functools
import heapq

import jax
import jax.numpy as jnp
from jax import lax
from jax.experimental import pallas as pl
from jax.experimental.pallas import tpu as pltpu
from jax.sharding import PartitionSpec as P

MESH = pl.DeviceIdType.MESH
SIZES = {"x": 4, "y": 4, "z": 8}
AXES = ("x", "y", "z")
ROWS, QUARTER, LANES = 16, 2048, 128
PARTS = {"A": ("xyz", 0, 4), "B": ("yzx", 4, 6), "C": ("zxy", 10, 6)}
STRAIGHT = {("A", 1): (2,), ("B", 1): (2,), ("C", 1): (3,)}
CUT = {("C", 3): 3}
READY = {"A": 0.0, "B": 0.9, "C": 1.6}
TILE_US, HOP_US, FAR_US, OP_US, LEAD_US = 0.089, 2.5, 0.65, 0.04, 0.8
OUTER = ("outer",)
OUTER_TILES = 32
FINISH_AFTER = 40


def messages():
    found = {}

    def chain(part, stage, tag, axis, region, start):
        _, low, tiles = PARTS[part]
        straight = STRAIGHT.get((part, stage), ())
        arrived = {0: start}
        base = (part, stage) + tag

        def add(name, step, far, place, first, last, after):
            spot = dict(region)
            spot[axis] = place
            found[base + name] = dict(
                part=part, stage=stage, link=(axis, step), far=far, region=spot,
                tiles=(low + first, low + last), after=list(after),
            )
            arrived.setdefault(place, []).append(base + name)
            return [base + name]

        if SIZES[axis] == 4:
            near = {step: add((step, 1), step, 1, step, 0, tiles, start) for step in (1, 3)}
            if 2 in straight:
                add((2, 2), 2, 2, 2, 0, tiles, start)
            else:
                cut = CUT.get((part, stage), tiles // 2)
                add((3, 2), 3, 1, 2, 0, cut, near[1])
                add((1, 2), 1, 1, 2, cut, tiles, near[3])
            return arrived
        half = SIZES[axis] // 2
        for sign, first, last in ((1, 0, tiles // 2), (-1, tiles // 2, tiles)):
            behind = {0: start}
            for hop in range(1, half + 1):
                back = 0 if hop in straight else hop - 1
                span = (0, tiles) if hop < half else (first, last)
                place = -sign * hop if hop < half else half
                behind[hop] = add((sign, hop), sign * (hop - back), hop - back, place, *span, behind[back])
        return arrived

    for part, (order, _, _) in PARTS.items():
        one, two, three = order
        firsts = chain(part, 1, (), one, {one: 0, two: 0, three: 0}, [("own", part)])
        seconds = {}
        for off, names in firsts.items():
            for place, news in chain(part, 2, (off,), two, {one: off, two: 0, three: 0}, names).items():
                if place != 0:
                    seconds.setdefault(place, []).extend(news)
        for off, names in firsts.items():
            chain(part, 3, (off, "one"), three, {one: off, two: 0, three: 0}, names)
        for off, names in seconds.items():
            chain(part, 3, (off, "all"), three, {one: None, two: off, three: 0}, names)
    found[OUTER] = dict(
        part=None, stage=4, link=("y", 1), far=1, region={}, tiles=(0, OUTER_TILES),
        after=[("own", part) for part in PARTS],
    )
    return found


def count(message):
    wide = 1
    for axis, place in message["region"].items():
        wide *= SIZES[axis] if place is None else 1
    return wide * (message["tiles"][1] - message["tiles"][0])


def forwards(found):
    groups = {}
    for name, message in found.items():
        part, stage, region = message["part"], message["stage"], message["region"]
        if part is None:
            continue
        order, low, tiles = PARTS[part]
        one, two, three = order
        key = (part, stage, region[two] if stage > 1 else 0, region[three] if stage > 2 else 0)
        groups.setdefault(key, ({one: None, two: key[2], three: key[3]}, (low, low + tiles), []))[2].append(name)
    for part in PARTS:
        groups[(part, 1, 0, 0)][2].append(("own", part))
    return list(groups.values())


def schedule(found, joined):
    users = {}
    for name, message in found.items():
        for before in message["after"]:
            users.setdefault(before, []).append(name)
    length = {name: count(message) * TILE_US for name, message in found.items()}
    delay = {name: HOP_US + FAR_US * (message["far"] - 1) for name, message in found.items()}
    remaining = {}

    def path(name):
        if name not in remaining:
            remaining[name] = length[name] + delay[name] + max([path(user) for user in users.get(name, [])] + [0.0])
        return remaining[name]

    def lanes(link):
        axis, step = link
        if axis == "z":
            return [((axis, 1 if step > 0 else -1), abs(step))]
        return [((axis, 1), 1), ((axis, 3), 1)] if step == 2 else [(link, 1)]

    needs = {name: len(message["after"]) for name, message in found.items()}
    cores = [set(names) for _, _, names in joined]
    arrivals = [(time, -1, ("own", part)) for part, time in READY.items()]
    heapq.heapify(arrivals)
    queues, free, steps = {}, {}, []
    clock, ticket = 0.0, 0
    while arrivals or any(queues.values()):
        if arrivals and arrivals[0][0] <= clock:
            what = heapq.heappop(arrivals)[2]
            clock += OP_US
            steps.append(("wait", what))
            for user in users.get(what, []):
                needs[user] -= 1
                if needs[user] == 0:
                    ticket += 1
                    heapq.heappush(queues.setdefault(found[user]["link"], []), (-path(user), ticket, user))
            for names in cores:
                names.discard(what)
            clock += OP_US * sum(1 for names in cores if not names)
            cores = [names for names in cores if names]
            continue
        backlog = {
            link: max(free.get(lane, 0.0) for lane, _ in lanes(link)) for link, queue in queues.items() if queue
        }
        open_links = [(max(until - clock, 0.0), link) for link, until in backlog.items() if until - clock < LEAD_US]
        if open_links:
            _, _, name = heapq.heappop(queues[min(open_links)[1]])
            clock += OP_US
            steps.append(("send", name))
            end = 0.0
            for lane, times in lanes(found[name]["link"]):
                free[lane] = max(clock, free.get(lane, 0.0)) + length[name] * times
                end = max(end, free[lane])
            ticket += 1
            heapq.heappush(arrivals, (end + delay[name], ticket, name))
            continue
        later = [until - LEAD_US + 1e-6 for until in backlog.values()]
        if arrivals:
            later.append(arrivals[0][0])
        clock = max(clock, min(later))
    return steps


def parity_table(rows, columns):
    i = lax.broadcasted_iota(jnp.int32, (rows, columns), 0)
    j = lax.broadcasted_iota(jnp.int32, (rows, columns), 1)
    both = jnp.bitwise_and(jnp.bitwise_and(i, j), LANES - 1)
    for shift in (4, 2, 1):
        both = jnp.bitwise_xor(both, jnp.right_shift(both, shift))
    return (1 - 2 * jnp.bitwise_and(both, 1)).astype(jnp.bfloat16)


def rotate(tiles, table):
    number, rows, lanes = tiles.shape
    flat = tiles.reshape(number * rows, lanes)
    high = flat.astype(jnp.bfloat16)
    low = (flat - high.astype(jnp.float32)).astype(jnp.bfloat16)
    flat = jnp.dot(jnp.concatenate([high, low], axis=1), table, preferred_element_type=jnp.float32)
    near = 1
    while near < number:
        pairs = flat.reshape(number // (2 * near), 2, near * rows, lanes)
        flat = jnp.concatenate(
            [(pairs[:, 0] + pairs[:, 1])[:, None], (pairs[:, 0] - pairs[:, 1])[:, None]], axis=1
        )
        near *= 2
    return flat.reshape(number, rows, lanes)


def exchange_kernel(
    steps, found, joined,
    lw_ref, base_ref, error_ref, momentum_ref, signs_ref, kept_ref,
    whole_ref, fresh_ref, dropped_ref,
    lw, base, error, momentum, signs, kept, part_sums, near, far, mine, outer,
    loads, near_send, near_recv, far_send, far_recv, outer_send, outer_recv,
    stage_send, message_recv, core_send, core_recv,
):
    rep, shard = lax.axis_index("rep"), lax.axis_index("shard")
    p, c = rep // 2, rep % 2
    x, y_high, z = (shard // 2) % 4, shard % 2, shard // 8
    block = base.shape[2]
    tiles_of_block = block // LANES

    def place_x(bits):
        return {0: x, 1: x + 1 - 2 * (x % 2), 2: (x + 2) % 4, 3: 3 - x}[bits]

    def place_y(bits):
        return (y_high if bits < 2 else 1 - y_high, p if bits % 2 == 0 else 1 - p)

    def place_z(step):
        return (z + step + SIZES["z"]) % SIZES["z"]

    def device(x_bits, y_bits, z_step, core):
        high, low = place_y(y_bits)
        return (low * 2 + core, place_z(z_step) * 8 + place_x(x_bits) * 2 + high)

    other_core = device(0, 0, 0, 1 - c)
    partner = device(0, 1, 0, c)

    def over(link):
        axis, step = link
        return device(step if axis == "x" else 0, step if axis == "y" else 0, step if axis == "z" else 0, c)

    copies = [pltpu.make_async_copy(signs_ref, signs, loads.at[0]), pltpu.make_async_copy(kept_ref, kept, loads.at[1])]
    for slot, b in enumerate((1 - p, p)):
        columns = pl.ds(pl.multiple_of(b * block, block), block)
        copies += [
            pltpu.make_async_copy(lw_ref.at[0, :, columns], lw.at[slot], loads.at[2 + 3 * slot]),
            pltpu.make_async_copy(base_ref.at[:, columns], base.at[slot], loads.at[3 + 3 * slot]),
            pltpu.make_async_copy(error_ref.at[0, :, columns], error.at[slot], loads.at[4 + 3 * slot]),
        ]
    copies.append(pltpu.make_async_copy(momentum_ref, momentum, loads.at[8]))
    for copy in copies:
        copy.start()

    barrier = pltpu.get_barrier_semaphore()
    peers = [over(link) for link in sorted({message["link"] for message in found.values()})] + [other_core]
    for target in peers:
        pl.semaphore_signal(barrier, inc=1, device_id=target, device_id_type=MESH)

    table = parity_table(2 * LANES, LANES)
    scale = 1.0 / 64.0

    def sketch(slot, b):
        for copy in copies[2 + 3 * slot:5 + 3 * slot]:
            copy.wait()
        compensated = (base[slot].astype(jnp.float32) - lw[slot].astype(jnp.float32)) + error[slot]
        comp = jnp.stack([compensated[:, t * LANES:(t + 1) * LANES] for t in range(tiles_of_block)])
        rows = pl.ds(pl.multiple_of(b * tiles_of_block, tiles_of_block), tiles_of_block)
        turn = signs[rows, :].astype(jnp.float32)[:, None, :]
        places = kept[pl.ds(b, 1), :]
        tile_hot = lax.broadcasted_iota(jnp.int32, (tiles_of_block, places.shape[1]), 0) == jnp.right_shift(places, 7)
        lane_hot = lax.broadcasted_iota(jnp.int32, (LANES, places.shape[1]), 0) == jnp.bitwise_and(places, LANES - 1)
        mask = lax.dot_general(
            tile_hot.astype(jnp.bfloat16), lane_hot.astype(jnp.bfloat16),
            (((1,), (1,)), ((), ())), preferred_element_type=jnp.float32,
        )[:, None, :]
        rotated = rotate(comp * turn, table) * scale
        back = rotate(jnp.where(mask > 0.5, rotated, 0.0), table) * (turn * scale)
        rest = comp - back
        half = tiles_of_block // 2
        for t in range(tiles_of_block):
            part_sums[2 * b + t // half, :, pl.ds((t % half) * LANES, LANES)] = back[t]
            dropped_ref[:, pl.ds(pl.multiple_of(b * block + t * LANES, LANES), LANES)] = rest[t]

    def remote(source, target, send, recv, where):
        return pltpu.make_async_remote_copy(
            src_ref=source, dst_ref=target, send_sem=send, recv_sem=recv, device_id=where, device_id_type=MESH
        )

    def at(region, tiles):
        every = slice(None)
        spot_x = every if region["x"] is None else place_x(region["x"])
        high, low = (every, every) if region["y"] is None else place_y(region["y"])
        spot_z = every if region["z"] is None else place_z(region["z"])
        return whole_ref.at[spot_z, spot_x, high, low, c, :, pl.ds(tiles[0] * LANES, (tiles[1] - tiles[0]) * LANES)]

    to_far = remote(part_sums.at[2 * (1 - p) + 1 - c], near.at[0], near_send.at[0], near_recv.at[0], other_core)
    to_mine = remote(part_sums.at[2 * p + 1 - c], near.at[1], near_send.at[1], near_recv.at[1], other_core)
    copies[0].wait()
    copies[1].wait()
    sketch(0, 1 - p)
    pl.semaphore_wait(barrier, len(peers))
    to_far.start()
    sketch(1, p)
    to_mine.start()
    to_far.wait_recv()
    pieces = {}
    for i, (part, (_, low, tiles)) in enumerate(PARTS.items()):
        columns = pl.ds(low * LANES, tiles * LANES)
        mine[:, columns] = part_sums[2 * (1 - p) + c, :, columns] + near[0, :, columns]
        pieces[part] = remote(mine.at[:, columns], far.at[:, columns], far_send.at[i], far_recv.at[i], partner)
        pieces[part].start()
    to_mine.wait_recv()
    copies[8].wait()

    names = {name: i for i, name in enumerate(name for name in found if name != OUTER)}
    sums = {(part, stage): 3 * i + stage - 1 for i, part in enumerate(PARTS) for stage in (1, 2, 3)}
    mine_outer, their_outer = outer.at[2 * p + c], outer.at[2 * (1 - p) + c]
    outer_far = remote(mine_outer, mine_outer, outer_send.at[0], outer_recv.at[0], partner)
    outer_near = remote(mine_outer, mine_outer, outer_send.at[1], outer_recv.at[1], other_core)
    outer_last = remote(their_outer, their_outer, outer_send.at[2], outer_recv.at[2], other_core)

    def moved(name, sender):
        message = found[name]
        axis, step = message["link"]
        region = dict(message["region"])
        if sender:
            region[axis] = region[axis] + step if axis == "z" else region[axis] ^ step
        place = at(region, message["tiles"])
        return remote(
            place, place, stage_send.at[sums[message["part"], message["stage"]]],
            message_recv.at[names[name]], over(message["link"]),
        )

    def own(part):
        _, low, tiles = PARTS[part]
        columns = pl.ds(low * LANES, tiles * LANES)
        pieces[part].wait_recv()
        total = (part_sums[2 * p + c, :, columns] + near[1, :, columns]) + far[:, columns]
        step = total * 0.25
        outer[2 * p + c, :, columns] = step
        wide = pl.ds(pl.multiple_of((2 * p + c) * QUARTER + low * LANES, LANES), tiles * LANES)
        fresh = 0.9 * momentum[:, wide] + step
        held = pl.ds(pl.multiple_of(c * QUARTER + low * LANES, LANES), tiles * LANES)
        lowered = base[1, :, held].astype(jnp.float32) - 0.7 * (step + 0.9 * fresh)
        whole_ref[z, x, y_high, p, c, :, columns] = lowered.astype(jnp.bfloat16)

    def finish():
        from_core = outer.at[2 * p + 1 - c]
        remote(from_core, from_core, outer_send.at[1], outer_recv.at[1], other_core).wait_recv()
        from_core = outer.at[2 * (1 - p) + 1 - c]
        remote(from_core, from_core, outer_send.at[2], outer_recv.at[2], other_core).wait_recv()
        for q in range(4):
            columns = pl.ds(q * QUARTER, QUARTER)
            fresh_ref[:, columns] = 0.9 * momentum[:, columns] + outer[q]

    waiting = [(set(group), region, tiles) for region, tiles, group in joined]
    outer_at = steps.index(("wait", OUTER))
    for i, (kind, what) in enumerate(steps):
        if i == outer_at + FINISH_AFTER:
            finish()
        if kind == "send":
            if what == OUTER:
                outer_far.start()
                outer_near.start()
            else:
                moved(what, True).start()
            continue
        if what == OUTER:
            remote(their_outer, their_outer, outer_send.at[0], outer_recv.at[0], partner).wait_recv()
            outer_last.start()
            continue
        if what[0] == "own":
            own(what[1])
        else:
            moved(what, False).wait_recv()
        for group, _, _ in waiting:
            group.discard(what)
        for _, region, tiles in [entry for entry in waiting if not entry[0]]:
            place = at(region, tiles)
            remote(place, place, core_send, core_recv, other_core).start()
        waiting = [entry for entry in waiting if entry[0]]
    if outer_at + FINISH_AFTER >= len(steps):
        finish()

    everything = whole_ref.at[:, :, :, :, 1 - c]
    remote(everything, everything, core_send, core_recv, other_core).wait_recv()
    everything = whole_ref.at[:, :, :, :, c]
    remote(everything, everything, core_send, core_recv, other_core).wait_send()
    for part, (order, low, tiles) in PARTS.items():
        columns = pl.ds(low * LANES, tiles * LANES)
        for stage in (1, 2, 3):
            ends = {axis: 1 for axis in AXES}
            for axis in order[:stage - 1]:
                ends[axis] = SIZES[axis]
            ends[order[stage - 1]] = SIZES[order[stage - 1]] - 1
            for high, low_y in {1: [(1, 1)], 3: [(1, 2), (1, 1)], 4: [(2, 2)]}[ends["y"]]:
                place = whole_ref.at[
                    pl.ds(0, ends["z"]), pl.ds(0, ends["x"]), pl.ds(0, high), pl.ds(0, low_y), c, :, columns
                ]
                remote(place, place, stage_send.at[sums[part, stage]], core_recv, other_core).wait_send()
    to_far.wait_send()
    to_mine.wait_send()
    for copy in list(pieces.values()) + [outer_far, outer_near, outer_last]:
        copy.wait_send()


def store_kernel(whole_ref, fresh_ref, dropped_ref, base_out, error_out, momentum_out, sems):
    copies = [
        pltpu.make_async_copy(fresh_ref, momentum_out, sems.at[0]),
        pltpu.make_async_copy(dropped_ref, error_out.at[0], sems.at[1]),
    ]
    for z in range(whole_ref.shape[0]):
        for low in range(2):
            for core in range(2):
                copies.append(pltpu.make_async_copy(
                    whole_ref.at[z, :, :, low, core],
                    base_out.at[z, :, :, :, pl.ds((2 * low + core) * QUARTER, QUARTER)],
                    sems.at[len(copies)],
                ))
    for copy in copies:
        copy.start()
    for copy in copies:
        copy.wait()


def shards(local_weights, base, error, momentum, signs, kept):
    rows, width = base.shape
    vmem = pl.BlockSpec(memory_space=pltpu.VMEM)
    hbm = pl.BlockSpec(memory_space=pl.ANY)
    held = lambda array: pltpu.with_memory_space_constraint(array, pltpu.VMEM)
    stay = lambda array: pltpu.with_memory_space_constraint(array, pltpu.HBM)
    found = messages()
    joined = forwards(found)
    steps = schedule(found, joined)
    dma = pltpu.SemaphoreType.DMA
    whole, fresh, dropped = pl.pallas_call(
        functools.partial(exchange_kernel, steps, found, joined),
        out_shape=(
            pltpu.VMEM((8, 4, 2, 2, 2, rows, QUARTER), jnp.bfloat16),
            pltpu.VMEM((rows, width), jnp.float32),
            pltpu.VMEM((rows, width), jnp.float32),
        ),
        in_specs=[hbm] * 6,
        out_specs=(vmem, vmem, vmem),
        scratch_shapes=[
            pltpu.VMEM((2, rows, width // 2), jnp.bfloat16),
            pltpu.VMEM((2, rows, width // 2), jnp.bfloat16),
            pltpu.VMEM((2, rows, width // 2), jnp.float32),
            pltpu.VMEM((rows, width), jnp.float32),
            pltpu.VMEM((width // LANES, LANES), jnp.int32),
            pltpu.VMEM(kept.shape, jnp.int32),
            pltpu.VMEM((4, rows, QUARTER), jnp.float32),
            pltpu.VMEM((2, rows, QUARTER), jnp.float32),
            pltpu.VMEM((rows, QUARTER), jnp.float32),
            pltpu.VMEM((rows, QUARTER), jnp.float32),
            pltpu.VMEM((4, rows, QUARTER), jnp.float32),
            dma((9,)), dma((2,)), dma((2,)), dma((3,)), dma((3,)), dma((3,)), dma((3,)),
            dma((9,)), dma((len(found) - 1,)), dma, dma,
        ],
        compiler_params=pltpu.CompilerParams(
            collective_id=0, has_side_effects=True, vmem_limit_bytes=16 << 20
        ),
        name="exchange",
    )(
        stay(local_weights), stay(base), stay(error), stay(momentum),
        stay(signs.reshape(width // LANES, LANES)), stay(kept),
    )

    new_base, new_error, new_momentum = pl.pallas_call(
        store_kernel,
        out_shape=(
            jax.ShapeDtypeStruct((8, 4, 2, rows, width), jnp.bfloat16),
            jax.ShapeDtypeStruct((1, rows, width), jnp.float32),
            jax.ShapeDtypeStruct((rows, width), jnp.float32),
        ),
        in_specs=[vmem] * 3,
        out_specs=(hbm, hbm, hbm),
        scratch_shapes=[dma((34,))],
        compiler_params=pltpu.CompilerParams(vmem_limit_bytes=16 << 20),
        name="store",
    )(held(whole), held(fresh), held(dropped))
    return (new_base.reshape(64 * rows, width), new_error, new_momentum)


def solution(mesh):
    in_specs = (
        P("rep", "shard", None),
        P("shard", None),
        P("rep", "shard", None),
        P("shard", None),
        P(),
        P(),
    )
    out_specs = (P(), P("rep", "shard", None), P("shard", None))
    return jax.shard_map(shards, mesh=mesh, in_specs=in_specs, out_specs=out_specs, check_vma=False)
```

```python
import functools
import heapq

import jax
import jax.numpy as jnp
from jax import lax
from jax.experimental import pallas as pl
from jax.experimental.pallas import tpu as pltpu
from jax.sharding import PartitionSpec as P

MESH = pl.DeviceIdType.MESH
SIZES = {"x": 4, "y": 4, "z": 8}
AXES = ("x", "y", "z")
ROWS, QUARTER, LANES = 16, 2048, 128
PARTS = {"A": ("xyz", 0, 4), "B": ("yzx", 4, 6), "C": ("zxy", 10, 6)}
STRAIGHT = {("A", 1): (2,), ("B", 1): (2,), ("C", 1): (3,)}
CUT = {("C", 3): 3}
SINGLES = {"A": (1, 1), "B": (1, 1), "C": (1, 1)}
READY = {"A": 0.0, "B": 0.9, "C": 1.6}
TILE_US, HOP_US, FAR_US, OP_US, LEAD_US = 0.092, 3.1, 0.65, 0.01, 0.4
OUTER = ("outer",)
OUTER_TILES = 32
FINISH_AFTER = 40


def messages():
    found, units = {}, {}

    def chain(part, stage, tag, axis, region, start):
        _, low, tiles = PARTS[part]
        straight = STRAIGHT.get((part, stage), ())
        arrived = {0: start}
        base = (part, stage) + tag
        half = SIZES[axis] // 2

        def add(name, step, far, place, first, last, after):
            spot = dict(region)
            spot[axis] = place
            unit = base + name
            whole = dict(spot)
            if place == half:
                unit = base + ("opposite",)
                if stage == 3 and tag[-1] == "one":
                    unit = (part, stage, "one", "opposite")
                    whole[PARTS[part][0][0]] = (0, 1)
            found[base + name] = dict(
                part=part, stage=stage, link=(axis, step), far=far, region=spot,
                tiles=(low + first, low + last), after=list(after), unit=unit,
            )
            units.setdefault(unit, (whole, (low, low + tiles), []))[2].append(base + name)
            if unit not in arrived.setdefault(place, []):
                arrived[place].append(unit)
            return [unit]

        if SIZES[axis] == 4:
            near = {step: add((step, 1), step, 1, step, 0, tiles, start) for step in (1, 3)}
            if 2 in straight:
                add((2, 2), 2, 2, 2, 0, tiles, start)
            else:
                cut = CUT.get((part, stage), tiles // 2)
                add((3, 2), 3, 1, 2, 0, cut, near[1])
                add((1, 2), 1, 1, 2, cut, tiles, near[3])
            return arrived
        for sign, first, last in ((1, 0, tiles // 2), (-1, tiles // 2, tiles)):
            behind = {0: start}
            for hop in range(1, half + 1):
                back = 0 if hop in straight else hop - 1
                span = (0, tiles) if hop < half else (first, last)
                place = -sign * hop if hop < half else half
                behind[hop] = add((sign, hop), sign * (hop - back), hop - back, place, *span, behind[back])
        return arrived

    for part, (order, _, _) in PARTS.items():
        one, two, three = order
        firsts = chain(part, 1, (), one, {one: 0, two: 0, three: 0}, [("own", part)])
        singles = [(off, {one: off, two: 0, three: 0}, names) for off, names in firsts.items()]
        together = [(9, {one: (0, 1), two: 0, three: 0}, [name for names in firsts.values() for name in names])]
        seconds = {}
        for off, region, names in singles if SINGLES[part][0] else together:
            for place, news in chain(part, 2, (off,), two, region, names).items():
                if place != 0:
                    seconds.setdefault(place, []).extend(news)
        for off, region, names in singles if SINGLES[part][1] else together:
            chain(part, 3, (off, "one"), three, region, names)
        for off, names in seconds.items():
            chain(part, 3, (off, "all"), three, {one: (0, 1), two: off, three: 0}, names)
    found[OUTER] = dict(
        part=None, stage=4, link=("y", 1), far=1, region={}, tiles=(0, OUTER_TILES),
        after=[("own", part) for part in PARTS], unit=OUTER,
    )
    units[OUTER] = ({}, None, [OUTER])
    return found, units


def count(region, tiles):
    wide = 1
    for axis, place in region.items():
        wide *= SIZES[axis] if isinstance(place, tuple) else 1
    return wide * (tiles[1] - tiles[0])


def forwards(found):
    groups = {}
    for message in found.values():
        part, stage, region = message["part"], message["stage"], message["region"]
        if part is None:
            continue
        order, low, tiles = PARTS[part]
        one, two, three = order
        key = (part, stage, region[two] if stage > 1 else 0, region[three] if stage > 2 else 0)
        entry = groups.setdefault(key, ({one: (0, 1), two: key[2], three: key[3]}, (low, low + tiles), set()))
        entry[2].add(message["unit"])
    for part in PARTS:
        groups[(part, 1, 0, 0)][2].add(("own", part))
    return list(groups.values())


def schedule(found, units, joined):
    users = {}
    for name, message in found.items():
        for before in message["after"]:
            users.setdefault(before, []).append(name)
    length = {name: count(message["region"], message["tiles"]) * TILE_US for name, message in found.items()}
    delay = {name: HOP_US + FAR_US * (message["far"] - 1) for name, message in found.items()}
    remaining = {}

    def path(name):
        if name not in remaining:
            after = [path(user) for user in users.get(found[name]["unit"], [])]
            remaining[name] = length[name] + delay[name] + max(after + [0.0])
        return remaining[name]

    def lanes(link):
        axis, step = link
        if axis == "z":
            return [((axis, 1 if step > 0 else -1), abs(step))]
        return [((axis, 1), 1), ((axis, 3), 1)] if step == 2 else [(link, 1)]

    needs = {name: len(message["after"]) for name, message in found.items()}
    flying = {unit: [len(names), 0.0] for unit, (_, _, names) in units.items()}
    cores = [set(names) for _, _, names in joined]
    arrivals = [(time, -1, ("own", part)) for part, time in READY.items()]
    heapq.heapify(arrivals)
    queues, free, steps = {}, {}, []
    clock, ticket = 0.0, 0
    while arrivals or any(queues.values()):
        if arrivals and arrivals[0][0] <= clock:
            what = heapq.heappop(arrivals)[2]
            clock += OP_US
            steps.append(("wait", what))
            for user in users.get(what, []):
                needs[user] -= 1
                if needs[user] == 0:
                    ticket += 1
                    heapq.heappush(queues.setdefault(found[user]["link"], []), (-path(user), ticket, user))
            for names in cores:
                names.discard(what)
            clock += OP_US * sum(1 for names in cores if not names)
            cores = [names for names in cores if names]
            continue
        backlog = {
            link: max(free.get(lane, 0.0) for lane, _ in lanes(link)) for link, queue in queues.items() if queue
        }
        open_links = [(max(until - clock, 0.0), link) for link, until in backlog.items() if until - clock < LEAD_US]
        if open_links:
            _, _, name = heapq.heappop(queues[min(open_links)[1]])
            clock += OP_US
            steps.append(("send", name))
            end = 0.0
            for lane, times in lanes(found[name]["link"]):
                free[lane] = max(clock, free.get(lane, 0.0)) + length[name] * times
                end = max(end, free[lane])
            flight = flying[found[name]["unit"]]
            flight[0] -= 1
            flight[1] = max(flight[1], end + delay[name])
            if flight[0] == 0:
                ticket += 1
                heapq.heappush(arrivals, (flight[1], ticket, found[name]["unit"]))
            continue
        later = [until - LEAD_US + 1e-6 for until in backlog.values()]
        if arrivals:
            later.append(arrivals[0][0])
        clock = max(clock, min(later))
    return steps


def parity_table(rows, columns):
    i = lax.broadcasted_iota(jnp.int32, (rows, columns), 0)
    j = lax.broadcasted_iota(jnp.int32, (rows, columns), 1)
    both = jnp.bitwise_and(jnp.bitwise_and(i, j), LANES - 1)
    for shift in (4, 2, 1):
        both = jnp.bitwise_xor(both, jnp.right_shift(both, shift))
    return (1 - 2 * jnp.bitwise_and(both, 1)).astype(jnp.bfloat16)


def rotate(tiles, table):
    number, rows, lanes = tiles.shape
    flat = tiles.reshape(number * rows, lanes)
    high = flat.astype(jnp.bfloat16)
    low = (flat - high.astype(jnp.float32)).astype(jnp.bfloat16)
    flat = jnp.dot(jnp.concatenate([high, low], axis=1), table, preferred_element_type=jnp.float32)
    near = 1
    while near < number:
        pairs = flat.reshape(number // (2 * near), 2, near * rows, lanes)
        flat = jnp.concatenate(
            [(pairs[:, 0] + pairs[:, 1])[:, None], (pairs[:, 0] - pairs[:, 1])[:, None]], axis=1
        )
        near *= 2
    return flat.reshape(number, rows, lanes)


def exchange_kernel(
    steps, found, units, joined,
    lw_ref, base_ref, error_ref, momentum_ref, signs_ref, kept_ref,
    whole_ref, fresh_ref, dropped_ref,
    lw, base, error, momentum, signs, kept, part_sums, near, far, mine, outer,
    loads, near_send, near_recv, far_send, far_recv, outer_send, outer_recv,
    stage_send, message_recv, core_send, core_recv,
):
    rep, shard = lax.axis_index("rep"), lax.axis_index("shard")
    p, c = rep // 2, rep % 2
    x, y_high, z = (shard // 2) % 4, shard % 2, shard // 8
    block = base.shape[2]
    tiles_of_block = block // LANES

    def place_x(bits):
        return {0: x, 1: x + 1 - 2 * (x % 2), 2: (x + 2) % 4, 3: 3 - x}[bits]

    def place_y(bits):
        return (y_high if bits < 2 else 1 - y_high, p if bits % 2 == 0 else 1 - p)

    def place_z(step):
        return (z + step + SIZES["z"]) % SIZES["z"]

    def device(x_bits, y_bits, z_step, core):
        high, low = place_y(y_bits)
        return (low * 2 + core, place_z(z_step) * 8 + place_x(x_bits) * 2 + high)

    other_core = device(0, 0, 0, 1 - c)
    partner = device(0, 1, 0, c)

    def over(link):
        axis, step = link
        return device(step if axis == "x" else 0, step if axis == "y" else 0, step if axis == "z" else 0, c)

    copies = [pltpu.make_async_copy(signs_ref, signs, loads.at[0]), pltpu.make_async_copy(kept_ref, kept, loads.at[1])]
    for slot, b in enumerate((1 - p, p)):
        columns = pl.ds(pl.multiple_of(b * block, block), block)
        copies += [
            pltpu.make_async_copy(lw_ref.at[0, :, columns], lw.at[slot], loads.at[2 + 3 * slot]),
            pltpu.make_async_copy(base_ref.at[:, columns], base.at[slot], loads.at[3 + 3 * slot]),
            pltpu.make_async_copy(error_ref.at[0, :, columns], error.at[slot], loads.at[4 + 3 * slot]),
        ]
    copies.append(pltpu.make_async_copy(momentum_ref, momentum, loads.at[8]))
    for copy in copies:
        copy.start()

    barrier = pltpu.get_barrier_semaphore()
    peers = [over(link) for link in sorted({message["link"] for message in found.values()})] + [other_core]
    for target in peers:
        pl.semaphore_signal(barrier, inc=1, device_id=target, device_id_type=MESH)

    table = parity_table(2 * LANES, LANES)
    scale = 1.0 / 64.0

    def sketch(slot, b):
        for copy in copies[2 + 3 * slot:5 + 3 * slot]:
            copy.wait()
        compensated = (base[slot].astype(jnp.float32) - lw[slot].astype(jnp.float32)) + error[slot]
        comp = jnp.stack([compensated[:, t * LANES:(t + 1) * LANES] for t in range(tiles_of_block)])
        rows = pl.ds(pl.multiple_of(b * tiles_of_block, tiles_of_block), tiles_of_block)
        turn = signs[rows, :].astype(jnp.float32)[:, None, :]
        places = kept[pl.ds(b, 1), :]
        tile_hot = lax.broadcasted_iota(jnp.int32, (tiles_of_block, places.shape[1]), 0) == jnp.right_shift(places, 7)
        lane_hot = lax.broadcasted_iota(jnp.int32, (LANES, places.shape[1]), 0) == jnp.bitwise_and(places, LANES - 1)
        mask = lax.dot_general(
            tile_hot.astype(jnp.bfloat16), lane_hot.astype(jnp.bfloat16),
            (((1,), (1,)), ((), ())), preferred_element_type=jnp.float32,
        )[:, None, :]
        rotated = rotate(comp * turn, table) * scale
        back = rotate(jnp.where(mask > 0.5, rotated, 0.0), table) * (turn * scale)
        rest = comp - back
        half = tiles_of_block // 2
        for t in range(tiles_of_block):
            part_sums[2 * b + t // half, :, pl.ds((t % half) * LANES, LANES)] = back[t]
            dropped_ref[:, pl.ds(pl.multiple_of(b * block + t * LANES, LANES), LANES)] = rest[t]

    def remote(source, target, send, recv, where):
        return pltpu.make_async_remote_copy(
            src_ref=source, dst_ref=target, send_sem=send, recv_sem=recv, device_id=where, device_id_type=MESH
        )

    def at(region, tiles):
        def span(axis):
            i, cuts = region[axis]
            wide = SIZES[axis] // cuts
            return pl.ds(i * wide, wide)

        spot_x = span("x") if isinstance(region["x"], tuple) else place_x(region["x"])
        spot_z = span("z") if isinstance(region["z"], tuple) else place_z(region["z"])
        if isinstance(region["y"], tuple):
            high, low = pl.ds(region["y"][0], 2 // region["y"][1]), slice(None)
        else:
            high, low = place_y(region["y"])
        return whole_ref.at[spot_z, spot_x, high, low, c, :, pl.ds(tiles[0] * LANES, (tiles[1] - tiles[0]) * LANES)]

    to_far = remote(part_sums.at[2 * (1 - p) + 1 - c], near.at[0], near_send.at[0], near_recv.at[0], other_core)
    to_mine = remote(part_sums.at[2 * p + 1 - c], near.at[1], near_send.at[1], near_recv.at[1], other_core)
    copies[0].wait()
    copies[1].wait()
    sketch(0, 1 - p)
    pl.semaphore_wait(barrier, len(peers))
    to_far.start()
    sketch(1, p)
    to_mine.start()
    to_far.wait_recv()
    pieces = {}
    for i, (part, (_, low, tiles)) in enumerate(PARTS.items()):
        columns = pl.ds(low * LANES, tiles * LANES)
        mine[:, columns] = part_sums[2 * (1 - p) + c, :, columns] + near[0, :, columns]
        pieces[part] = remote(mine.at[:, columns], far.at[:, columns], far_send.at[i], far_recv.at[i], partner)
        pieces[part].start()
    to_mine.wait_recv()
    copies[8].wait()

    spots = {unit: i for i, unit in enumerate(unit for unit in units if unit != OUTER)}
    sums = {(part, stage): 3 * i + stage - 1 for i, part in enumerate(PARTS) for stage in (1, 2, 3)}
    mine_outer, their_outer = outer.at[2 * p + c], outer.at[2 * (1 - p) + c]
    outer_far = remote(mine_outer, mine_outer, outer_send.at[0], outer_recv.at[0], partner)
    outer_near = remote(mine_outer, mine_outer, outer_send.at[1], outer_recv.at[1], other_core)
    outer_last = remote(their_outer, their_outer, outer_send.at[2], outer_recv.at[2], other_core)

    def send(name):
        message = found[name]
        axis, step = message["link"]
        region = dict(message["region"])
        region[axis] = region[axis] + step if axis == "z" else region[axis] ^ step
        place = at(region, message["tiles"])
        remote(
            place, place, stage_send.at[sums[message["part"], message["stage"]]],
            message_recv.at[spots[message["unit"]]], over(message["link"]),
        ).start()

    def take(unit):
        region, tiles, _ = units[unit]
        place = at(region, tiles)
        remote(place, place, core_send, message_recv.at[spots[unit]], other_core).wait_recv()

    def own(part):
        _, low, tiles = PARTS[part]
        columns = pl.ds(low * LANES, tiles * LANES)
        pieces[part].wait_recv()
        total = (part_sums[2 * p + c, :, columns] + near[1, :, columns]) + far[:, columns]
        step = total * 0.25
        outer[2 * p + c, :, columns] = step
        wide = pl.ds(pl.multiple_of((2 * p + c) * QUARTER + low * LANES, LANES), tiles * LANES)
        fresh = 0.9 * momentum[:, wide] + step
        held = pl.ds(pl.multiple_of(c * QUARTER + low * LANES, LANES), tiles * LANES)
        lowered = base[1, :, held].astype(jnp.float32) - 0.7 * (step + 0.9 * fresh)
        whole_ref[z, x, y_high, p, c, :, columns] = lowered.astype(jnp.bfloat16)

    def finish():
        from_core = outer.at[2 * p + 1 - c]
        remote(from_core, from_core, outer_send.at[1], outer_recv.at[1], other_core).wait_recv()
        from_core = outer.at[2 * (1 - p) + 1 - c]
        remote(from_core, from_core, outer_send.at[2], outer_recv.at[2], other_core).wait_recv()
        for q in range(4):
            columns = pl.ds(q * QUARTER, QUARTER)
            fresh_ref[:, columns] = 0.9 * momentum[:, columns] + outer[q]

    waiting = [(set(group), region, tiles) for region, tiles, group in joined]
    outer_at = steps.index(("wait", OUTER))
    for i, (kind, what) in enumerate(steps):
        if i == outer_at + FINISH_AFTER:
            finish()
        if kind == "send":
            if what == OUTER:
                outer_far.start()
                outer_near.start()
            else:
                send(what)
            continue
        if what == OUTER:
            remote(their_outer, their_outer, outer_send.at[0], outer_recv.at[0], partner).wait_recv()
            outer_last.start()
            continue
        if what[0] == "own":
            own(what[1])
        else:
            take(what)
        for group, _, _ in waiting:
            group.discard(what)
        for _, region, tiles in [entry for entry in waiting if not entry[0]]:
            place = at(region, tiles)
            remote(place, place, core_send, core_recv, other_core).start()
        waiting = [entry for entry in waiting if entry[0]]
    if outer_at + FINISH_AFTER >= len(steps):
        finish()

    for part, (order, low, tiles) in PARTS.items():
        columns = pl.ds(low * LANES, tiles * LANES)
        for stage in (1, 2, 3):
            ends = {axis: 1 for axis in AXES}
            for axis in order[:stage - 1]:
                ends[axis] = SIZES[axis]
            ends[order[stage - 1]] = SIZES[order[stage - 1]] - 1
            for high, low_y in {1: [(1, 1)], 3: [(1, 2), (1, 1)], 4: [(2, 2)]}[ends["y"]]:
                place = whole_ref.at[
                    pl.ds(0, ends["z"]), pl.ds(0, ends["x"]), pl.ds(0, high), pl.ds(0, low_y), c, :, columns
                ]
                remote(place, place, stage_send.at[sums[part, stage]], core_recv, other_core).wait_send()
    to_far.wait_send()
    to_mine.wait_send()
    for copy in list(pieces.values()) + [outer_far, outer_near, outer_last]:
        copy.wait_send()
    everything = whole_ref.at[:, :, :, :, c]
    remote(everything, everything, core_send, core_recv, other_core).wait_send()
    everything = whole_ref.at[:, :, :, :, 1 - c]
    remote(everything, everything, core_send, core_recv, other_core).wait_recv()


def store_kernel(whole_ref, fresh_ref, dropped_ref, base_out, error_out, momentum_out, sems):
    copies = [
        pltpu.make_async_copy(fresh_ref, momentum_out, sems.at[0]),
        pltpu.make_async_copy(dropped_ref, error_out.at[0], sems.at[1]),
    ]
    for z in range(whole_ref.shape[0]):
        for low in range(2):
            for core in range(2):
                copies.append(pltpu.make_async_copy(
                    whole_ref.at[z, :, :, low, core],
                    base_out.at[z, :, :, :, pl.ds((2 * low + core) * QUARTER, QUARTER)],
                    sems.at[len(copies)],
                ))
    for copy in copies:
        copy.start()
    for copy in copies:
        copy.wait()


def shards(local_weights, base, error, momentum, signs, kept):
    rows, width = base.shape
    vmem = pl.BlockSpec(memory_space=pltpu.VMEM)
    hbm = pl.BlockSpec(memory_space=pl.ANY)
    held = lambda array: pltpu.with_memory_space_constraint(array, pltpu.VMEM)
    stay = lambda array: pltpu.with_memory_space_constraint(array, pltpu.HBM)
    found, units = messages()
    joined = forwards(found)
    steps = schedule(found, units, joined)
    dma = pltpu.SemaphoreType.DMA
    whole, fresh, dropped = pl.pallas_call(
        functools.partial(exchange_kernel, steps, found, units, joined),
        out_shape=(
            pltpu.VMEM((8, 4, 2, 2, 2, rows, QUARTER), jnp.bfloat16),
            pltpu.VMEM((rows, width), jnp.float32),
            pltpu.VMEM((rows, width), jnp.float32),
        ),
        in_specs=[hbm] * 6,
        out_specs=(vmem, vmem, vmem),
        scratch_shapes=[
            pltpu.VMEM((2, rows, width // 2), jnp.bfloat16),
            pltpu.VMEM((2, rows, width // 2), jnp.bfloat16),
            pltpu.VMEM((2, rows, width // 2), jnp.float32),
            pltpu.VMEM((rows, width), jnp.float32),
            pltpu.VMEM((width // LANES, LANES), jnp.int32),
            pltpu.VMEM(kept.shape, jnp.int32),
            pltpu.VMEM((4, rows, QUARTER), jnp.float32),
            pltpu.VMEM((2, rows, QUARTER), jnp.float32),
            pltpu.VMEM((rows, QUARTER), jnp.float32),
            pltpu.VMEM((rows, QUARTER), jnp.float32),
            pltpu.VMEM((4, rows, QUARTER), jnp.float32),
            dma((9,)), dma((2,)), dma((2,)), dma((3,)), dma((3,)), dma((3,)), dma((3,)),
            dma((9,)), dma((len(units) - 1,)), dma, dma,
        ],
        compiler_params=pltpu.CompilerParams(
            collective_id=0, has_side_effects=True, vmem_limit_bytes=16 << 20
        ),
        name="exchange",
    )(
        stay(local_weights), stay(base), stay(error), stay(momentum),
        stay(signs.reshape(width // LANES, LANES)), stay(kept),
    )

    new_base, new_error, new_momentum = pl.pallas_call(
        store_kernel,
        out_shape=(
            jax.ShapeDtypeStruct((8, 4, 2, rows, width), jnp.bfloat16),
            jax.ShapeDtypeStruct((1, rows, width), jnp.float32),
            jax.ShapeDtypeStruct((rows, width), jnp.float32),
        ),
        in_specs=[vmem] * 3,
        out_specs=(hbm, hbm, hbm),
        scratch_shapes=[dma((34,))],
        compiler_params=pltpu.CompilerParams(vmem_limit_bytes=16 << 20),
        name="store",
    )(held(whole), held(fresh), held(dropped))
    return (new_base.reshape(64 * rows, width), new_error, new_momentum)


def solution(mesh):
    in_specs = (
        P("rep", "shard", None),
        P("shard", None),
        P("rep", "shard", None),
        P("shard", None),
        P(),
        P(),
    )
    out_specs = (P(), P("rep", "shard", None), P("shard", None))
    return jax.shard_map(shards, mesh=mesh, in_specs=in_specs, out_specs=out_specs, check_vma=False)
```

```python
import functools
import heapq

import jax
import jax.numpy as jnp
from jax import lax
from jax.experimental import pallas as pl
from jax.experimental.pallas import tpu as pltpu
from jax.sharding import PartitionSpec as P

MESH = pl.DeviceIdType.MESH
SIZES = {"x": 4, "y": 4, "z": 8}
AXES = ("x", "y", "z")
ROWS, QUARTER, LANES = 16, 2048, 128
PARTS = {"A": ("zxy", 0, 5), "B": ("zyx", 5, 6), "C": ("xyz", 11, 5)}
STRAIGHT = {("A", 1): (2,), ("B", 1): (3,), ("C", 1): (2,)}
CUT = {("A", 3): 3}
SINGLES = {"A": (1, 1), "B": (1, 1), "C": (0, 1)}
TILE_US, HOP_US, FAR_US, OP_US, LEAD_US = 0.092, 3.1, 0.65, 0.01, 0.8
OUTER = ("outer",)
OUTER_TILES = 32
FINISH_AFTER = 40


def messages():
    found, units = {}, {}

    def chain(part, stage, tag, axis, region, start):
        _, low, tiles = PARTS[part]
        straight = STRAIGHT.get((part, stage), ())
        arrived = {0: start}
        base = (part, stage) + tag
        half = SIZES[axis] // 2

        def add(name, step, far, place, first, last, after):
            spot = dict(region)
            spot[axis] = place
            unit = base + name
            whole = dict(spot)
            if place == half:
                unit = base + ("opposite",)
                if stage == 3 and tag[-1] == "one":
                    unit = (part, stage, "one", "opposite")
                    whole[PARTS[part][0][0]] = (0, 1)
            found[base + name] = dict(
                part=part, stage=stage, link=(axis, step), far=far, region=spot,
                tiles=(low + first, low + last), after=list(after), unit=unit,
            )
            units.setdefault(unit, (whole, (low, low + tiles), []))[2].append(base + name)
            if unit not in arrived.setdefault(place, []):
                arrived[place].append(unit)
            return [unit]

        if SIZES[axis] == 4:
            near = {step: add((step, 1), step, 1, step, 0, tiles, start) for step in (1, 3)}
            if 2 in straight:
                add((2, 2), 2, 2, 2, 0, tiles, start)
            else:
                cut = CUT.get((part, stage), tiles // 2)
                add((3, 2), 3, 1, 2, 0, cut, near[1])
                add((1, 2), 1, 1, 2, cut, tiles, near[3])
            return arrived
        for sign, first, last in ((1, 0, tiles // 2), (-1, tiles // 2, tiles)):
            behind = {0: start}
            for hop in range(1, half + 1):
                back = 0 if hop in straight else hop - 1
                span = (0, tiles) if hop < half else (first, last)
                place = -sign * hop if hop < half else half
                behind[hop] = add((sign, hop), sign * (hop - back), hop - back, place, *span, behind[back])
        return arrived

    for part, (order, _, _) in PARTS.items():
        one, two, three = order
        firsts = chain(part, 1, (), one, {one: 0, two: 0, three: 0}, [("own", part)])
        singles = [(off, {one: off, two: 0, three: 0}, names) for off, names in firsts.items()]
        together = [(9, {one: (0, 1), two: 0, three: 0}, [name for names in firsts.values() for name in names])]
        seconds = {}
        for off, region, names in singles if SINGLES[part][0] else together:
            for place, news in chain(part, 2, (off,), two, region, names).items():
                if place != 0:
                    seconds.setdefault(place, []).extend(news)
        for off, region, names in singles if SINGLES[part][1] else together:
            chain(part, 3, (off, "one"), three, region, names)
        for off, names in seconds.items():
            chain(part, 3, (off, "all"), three, {one: (0, 1), two: off, three: 0}, names)
    found[OUTER] = dict(
        part=None, stage=4, link=("y", 1), far=1, region={}, tiles=(0, OUTER_TILES),
        after=[("own", part) for part in PARTS], unit=OUTER,
    )
    units[OUTER] = ({}, None, [OUTER])
    return found, units


def count(region, tiles):
    wide = 1
    for axis, place in region.items():
        wide *= SIZES[axis] if isinstance(place, tuple) else 1
    return wide * (tiles[1] - tiles[0])


def forwards(found):
    groups = {}
    for message in found.values():
        part, stage, region = message["part"], message["stage"], message["region"]
        if part is None:
            continue
        order, low, tiles = PARTS[part]
        one, two, three = order
        key = (part, stage, region[two] if stage > 1 else 0, region[three] if stage > 2 else 0)
        entry = groups.setdefault(key, ({one: (0, 1), two: key[2], three: key[3]}, (low, low + tiles), set()))
        entry[2].add(message["unit"])
    for part in PARTS:
        groups[(part, 1, 0, 0)][2].add(("own", part))
    return list(groups.values())


def schedule(found, units, joined):
    users = {}
    for name, message in found.items():
        for before in message["after"]:
            users.setdefault(before, []).append(name)
    length = {name: count(message["region"], message["tiles"]) * TILE_US for name, message in found.items()}
    delay = {name: HOP_US + FAR_US * (message["far"] - 1) for name, message in found.items()}
    remaining = {}

    def path(name):
        if name not in remaining:
            after = [path(user) for user in users.get(found[name]["unit"], [])]
            remaining[name] = length[name] + delay[name] + max(after + [0.0])
        return remaining[name]

    def lanes(link):
        axis, step = link
        if axis == "z":
            return [((axis, 1 if step > 0 else -1), abs(step))]
        return [((axis, 1), 1), ((axis, 3), 1)] if step == 2 else [(link, 1)]

    needs = {name: len(message["after"]) for name, message in found.items()}
    flying = {unit: [len(names), 0.0] for unit, (_, _, names) in units.items()}
    cores = [set(names) for _, _, names in joined]
    arrivals = [(2 * (low + tiles) * TILE_US, -1, ("own", part)) for part, (_, low, tiles) in PARTS.items()]
    heapq.heapify(arrivals)
    queues, free, steps = {}, {}, []
    clock, ticket = 0.0, 0
    while arrivals or any(queues.values()):
        if arrivals and arrivals[0][0] <= clock:
            what = heapq.heappop(arrivals)[2]
            clock += OP_US
            steps.append(("wait", what))
            for user in users.get(what, []):
                needs[user] -= 1
                if needs[user] == 0:
                    ticket += 1
                    heapq.heappush(queues.setdefault(found[user]["link"], []), (-path(user), ticket, user))
            for names in cores:
                names.discard(what)
            clock += OP_US * sum(1 for names in cores if not names)
            cores = [names for names in cores if names]
            continue
        backlog = {
            link: max(free.get(lane, 0.0) for lane, _ in lanes(link)) for link, queue in queues.items() if queue
        }
        open_links = [(max(until - clock, 0.0), link) for link, until in backlog.items() if until - clock < LEAD_US]
        if open_links:
            _, _, name = heapq.heappop(queues[min(open_links)[1]])
            clock += OP_US
            steps.append(("send", name))
            end = 0.0
            for lane, times in lanes(found[name]["link"]):
                free[lane] = max(clock, free.get(lane, 0.0)) + length[name] * times
                end = max(end, free[lane])
            flight = flying[found[name]["unit"]]
            flight[0] -= 1
            flight[1] = max(flight[1], end + delay[name])
            if flight[0] == 0:
                ticket += 1
                heapq.heappush(arrivals, (flight[1], ticket, found[name]["unit"]))
            continue
        later = [until - LEAD_US + 1e-6 for until in backlog.values()]
        if arrivals:
            later.append(arrivals[0][0])
        clock = max(clock, min(later))
    return steps


def share(found, units, steps):
    at = {step: i for i, step in enumerate(steps)}
    links = {}
    for name, message in found.items():
        if message["part"] is not None:
            links.setdefault(message["link"], []).append((at["send", name], at["wait", message["unit"]]))

    def known(unit, name):
        axis, step = found[name]["link"]
        back = (axis, -step) if axis == "z" else (axis, step)
        over = at["wait", unit]
        return any(sent > over and taken < at["send", name] for sent, taken in links.get(back, []))

    spots, last = {}, []
    rest = [unit for unit in units if unit != OUTER]
    for unit in sorted(rest, key=lambda unit: min(at["send", name] for name in units[unit][2])):
        free = [i for i, old in enumerate(last) if all(known(old, name) for name in units[unit][2])]
        if free:
            spots[unit] = max(free, key=lambda i: at["wait", last[i]])
            last[spots[unit]] = unit
        else:
            spots[unit] = len(last)
            last.append(unit)
    return spots, len(last)


def parity_table(rows, columns):
    i = lax.broadcasted_iota(jnp.int32, (rows, columns), 0)
    j = lax.broadcasted_iota(jnp.int32, (rows, columns), 1)
    both = jnp.bitwise_and(jnp.bitwise_and(i, j), LANES - 1)
    for shift in (4, 2, 1):
        both = jnp.bitwise_xor(both, jnp.right_shift(both, shift))
    return (1 - 2 * jnp.bitwise_and(both, 1)).astype(jnp.bfloat16)


def rotate(tiles, table):
    number, rows, lanes = tiles.shape
    flat = tiles.reshape(number * rows, lanes)
    high = flat.astype(jnp.bfloat16)
    low = (flat - high.astype(jnp.float32)).astype(jnp.bfloat16)
    flat = jnp.dot(jnp.concatenate([high, low], axis=1), table, preferred_element_type=jnp.float32)
    near = 1
    while near < number:
        pairs = flat.reshape(number // (2 * near), 2, near * rows, lanes)
        flat = jnp.concatenate(
            [(pairs[:, 0] + pairs[:, 1])[:, None], (pairs[:, 0] - pairs[:, 1])[:, None]], axis=1
        )
        near *= 2
    return flat.reshape(number, rows, lanes)


def exchange_kernel(
    steps, found, units, joined, spots,
    lw_ref, base_ref, error_ref, momentum_ref, signs_ref, kept_ref,
    whole_ref, fresh_ref, dropped_ref,
    lw, base, error, momentum, signs, kept, part_sums, near, far, mine, outer,
    loads, near_send, near_recv, far_send, far_recv, outer_send, outer_recv,
    all_send, message_recv, core_send, core_recv,
):
    rep, shard = lax.axis_index("rep"), lax.axis_index("shard")
    p, c = rep // 2, rep % 2
    x, y_high, z = (shard // 2) % 4, shard % 2, shard // 8
    block = base.shape[2]
    tiles_of_block = block // LANES

    def place_x(bits):
        return {0: x, 1: x + 1 - 2 * (x % 2), 2: (x + 2) % 4, 3: 3 - x}[bits]

    def place_y(bits):
        return (y_high if bits < 2 else 1 - y_high, p if bits % 2 == 0 else 1 - p)

    def place_z(step):
        return (z + step + SIZES["z"]) % SIZES["z"]

    def device(x_bits, y_bits, z_step, core):
        high, low = place_y(y_bits)
        return (low * 2 + core, place_z(z_step) * 8 + place_x(x_bits) * 2 + high)

    other_core = device(0, 0, 0, 1 - c)
    partner = device(0, 1, 0, c)

    def over(link):
        axis, step = link
        return device(step if axis == "x" else 0, step if axis == "y" else 0, step if axis == "z" else 0, c)

    copies = [pltpu.make_async_copy(signs_ref, signs, loads.at[0]), pltpu.make_async_copy(kept_ref, kept, loads.at[1])]
    for slot, b in enumerate((1 - p, p)):
        columns = pl.ds(pl.multiple_of(b * block, block), block)
        copies += [
            pltpu.make_async_copy(lw_ref.at[0, :, columns], lw.at[slot], loads.at[2 + 3 * slot]),
            pltpu.make_async_copy(base_ref.at[:, columns], base.at[slot], loads.at[3 + 3 * slot]),
            pltpu.make_async_copy(error_ref.at[0, :, columns], error.at[slot], loads.at[4 + 3 * slot]),
        ]
    copies.append(pltpu.make_async_copy(momentum_ref, momentum, loads.at[8]))
    for copy in copies:
        copy.start()

    barrier = pltpu.get_barrier_semaphore()
    peers = [over(link) for link in sorted({message["link"] for message in found.values()})] + [other_core]
    for target in peers:
        pl.semaphore_signal(barrier, inc=1, device_id=target, device_id_type=MESH)

    table = parity_table(2 * LANES, LANES)
    scale = 1.0 / 64.0

    def kept_mask(b):
        places = kept[pl.ds(b, 1), :]
        tile_hot = lax.broadcasted_iota(jnp.int32, (tiles_of_block, places.shape[1]), 0) == jnp.right_shift(places, 7)
        lane_hot = lax.broadcasted_iota(jnp.int32, (LANES, places.shape[1]), 0) == jnp.bitwise_and(places, LANES - 1)
        return lax.dot_general(
            tile_hot.astype(jnp.bfloat16), lane_hot.astype(jnp.bfloat16),
            (((1,), (1,)), ((), ())), preferred_element_type=jnp.float32,
        )[:, None, :]

    def sketch(slot, b, mask):
        for copy in copies[2 + 3 * slot:5 + 3 * slot]:
            copy.wait()
        compensated = (base[slot].astype(jnp.float32) - lw[slot].astype(jnp.float32)) + error[slot]
        comp = jnp.stack([compensated[:, t * LANES:(t + 1) * LANES] for t in range(tiles_of_block)])
        rows = pl.ds(pl.multiple_of(b * tiles_of_block, tiles_of_block), tiles_of_block)
        turn = signs[rows, :].astype(jnp.float32)[:, None, :]
        rotated = rotate(comp * turn, table) * scale
        back = rotate(jnp.where(mask > 0.5, rotated, 0.0), table) * (turn * scale)
        rest = comp - back
        half = tiles_of_block // 2
        for t in range(tiles_of_block):
            part_sums[2 * b + t // half, :, pl.ds((t % half) * LANES, LANES)] = back[t]
            dropped_ref[:, pl.ds(pl.multiple_of(b * block + t * LANES, LANES), LANES)] = rest[t]

    def remote(source, target, send, recv, where):
        return pltpu.make_async_remote_copy(
            src_ref=source, dst_ref=target, send_sem=send, recv_sem=recv, device_id=where, device_id_type=MESH
        )

    def at(region, tiles):
        def span(axis):
            i, cuts = region[axis]
            wide = SIZES[axis] // cuts
            return pl.ds(i * wide, wide)

        spot_x = span("x") if isinstance(region["x"], tuple) else place_x(region["x"])
        spot_z = span("z") if isinstance(region["z"], tuple) else place_z(region["z"])
        if isinstance(region["y"], tuple):
            high, low = pl.ds(region["y"][0], 2 // region["y"][1]), slice(None)
        else:
            high, low = place_y(region["y"])
        return whole_ref.at[spot_z, spot_x, high, low, c, :, pl.ds(tiles[0] * LANES, (tiles[1] - tiles[0]) * LANES)]

    to_far = remote(part_sums.at[2 * (1 - p) + 1 - c], near.at[0], near_send.at[0], near_recv.at[0], other_core)
    to_mine = remote(part_sums.at[2 * p + 1 - c], near.at[1], near_send.at[1], near_recv.at[1], other_core)
    copies[0].wait()
    copies[1].wait()
    first_mask = kept_mask(1 - p)
    sketch(0, 1 - p, first_mask)
    pl.semaphore_wait(barrier, len(peers))
    to_far.start()
    sketch(1, p, kept_mask(p))
    to_mine.start()
    to_far.wait_recv()
    pieces = {}
    for i, (part, (_, low, tiles)) in enumerate(PARTS.items()):
        columns = pl.ds(low * LANES, tiles * LANES)
        mine[:, columns] = part_sums[2 * (1 - p) + c, :, columns] + near[0, :, columns]
        pieces[part] = remote(mine.at[:, columns], far.at[:, columns], far_send.at[i], far_recv.at[i], partner)
        pieces[part].start()
    to_mine.wait_recv()
    copies[8].wait()

    mine_outer, their_outer = outer.at[2 * p + c], outer.at[2 * (1 - p) + c]
    outer_far = remote(mine_outer, mine_outer, outer_send.at[0], outer_recv.at[0], partner)
    outer_near = remote(mine_outer, mine_outer, outer_send.at[1], outer_recv.at[1], other_core)
    outer_last = remote(their_outer, their_outer, outer_send.at[2], outer_recv.at[2], other_core)

    def send(name):
        message = found[name]
        axis, step = message["link"]
        region = dict(message["region"])
        region[axis] = region[axis] + step if axis == "z" else region[axis] ^ step
        place = at(region, message["tiles"])
        remote(
            place, place, all_send, message_recv.at[spots[message["unit"]]], over(message["link"]),
        ).start()

    def take(unit):
        region, tiles, _ = units[unit]
        place = at(region, tiles)
        remote(place, place, core_send, message_recv.at[spots[unit]], other_core).wait_recv()

    def own(part):
        _, low, tiles = PARTS[part]
        columns = pl.ds(low * LANES, tiles * LANES)
        pieces[part].wait_recv()
        total = (part_sums[2 * p + c, :, columns] + near[1, :, columns]) + far[:, columns]
        step = total * 0.25
        outer[2 * p + c, :, columns] = step
        wide = pl.ds(pl.multiple_of((2 * p + c) * QUARTER + low * LANES, LANES), tiles * LANES)
        fresh = 0.9 * momentum[:, wide] + step
        held = pl.ds(pl.multiple_of(c * QUARTER + low * LANES, LANES), tiles * LANES)
        lowered = base[1, :, held].astype(jnp.float32) - 0.7 * (step + 0.9 * fresh)
        whole_ref[z, x, y_high, p, c, :, columns] = lowered.astype(jnp.bfloat16)

    def finish():
        from_core = outer.at[2 * p + 1 - c]
        remote(from_core, from_core, outer_send.at[1], outer_recv.at[1], other_core).wait_recv()
        from_core = outer.at[2 * (1 - p) + 1 - c]
        remote(from_core, from_core, outer_send.at[2], outer_recv.at[2], other_core).wait_recv()
        for q in range(4):
            columns = pl.ds(q * QUARTER, QUARTER)
            fresh_ref[:, columns] = 0.9 * momentum[:, columns] + outer[q]

    waiting = [(set(group), region, tiles) for region, tiles, group in joined]
    outer_at = steps.index(("wait", OUTER))
    for i, (kind, what) in enumerate(steps):
        if i == outer_at + FINISH_AFTER:
            finish()
        if kind == "send":
            if what == OUTER:
                outer_far.start()
                outer_near.start()
            else:
                send(what)
            continue
        if what == OUTER:
            remote(their_outer, their_outer, outer_send.at[0], outer_recv.at[0], partner).wait_recv()
            outer_last.start()
            continue
        if what[0] == "own":
            own(what[1])
        else:
            take(what)
        for group, _, _ in waiting:
            group.discard(what)
        for _, region, tiles in [entry for entry in waiting if not entry[0]]:
            place = at(region, tiles)
            remote(place, place, core_send, core_recv, other_core).start()
        waiting = [entry for entry in waiting if entry[0]]
    if outer_at + FINISH_AFTER >= len(steps):
        finish()

    for part, (order, low, tiles) in PARTS.items():
        columns = pl.ds(low * LANES, tiles * LANES)
        for stage in (1, 2, 3):
            ends = {axis: 1 for axis in AXES}
            for axis in order[:stage - 1]:
                ends[axis] = SIZES[axis]
            ends[order[stage - 1]] = SIZES[order[stage - 1]] - 1
            for high, low_y in {1: [(1, 1)], 3: [(1, 2), (1, 1)], 4: [(2, 2)]}[ends["y"]]:
                place = whole_ref.at[
                    pl.ds(0, ends["z"]), pl.ds(0, ends["x"]), pl.ds(0, high), pl.ds(0, low_y), c, :, columns
                ]
                remote(place, place, all_send, core_recv, other_core).wait_send()
    to_far.wait_send()
    to_mine.wait_send()
    for copy in list(pieces.values()) + [outer_far, outer_near, outer_last]:
        copy.wait_send()
    everything = whole_ref.at[:, :, :, :, c]
    remote(everything, everything, core_send, core_recv, other_core).wait_send()
    everything = whole_ref.at[:, :, :, :, 1 - c]
    remote(everything, everything, core_send, core_recv, other_core).wait_recv()


def store_kernel(whole_ref, fresh_ref, dropped_ref, base_out, error_out, momentum_out, sems):
    copies = [
        pltpu.make_async_copy(fresh_ref, momentum_out, sems.at[0]),
        pltpu.make_async_copy(dropped_ref, error_out.at[0], sems.at[1]),
    ]
    for z in range(whole_ref.shape[0]):
        for low in range(2):
            for core in range(2):
                copies.append(pltpu.make_async_copy(
                    whole_ref.at[z, :, :, low, core],
                    base_out.at[z, :, :, :, pl.ds((2 * low + core) * QUARTER, QUARTER)],
                    sems.at[len(copies)],
                ))
    for copy in copies:
        copy.start()
    for copy in copies:
        copy.wait()


def shards(local_weights, base, error, momentum, signs, kept):
    rows, width = base.shape
    vmem = pl.BlockSpec(memory_space=pltpu.VMEM)
    hbm = pl.BlockSpec(memory_space=pl.ANY)
    held = lambda array: pltpu.with_memory_space_constraint(array, pltpu.VMEM)
    stay = lambda array: pltpu.with_memory_space_constraint(array, pltpu.HBM)
    found, units = messages()
    joined = forwards(found)
    steps = schedule(found, units, joined)
    spots, number = share(found, units, steps)
    dma = pltpu.SemaphoreType.DMA
    whole, fresh, dropped = pl.pallas_call(
        functools.partial(exchange_kernel, steps, found, units, joined, spots),
        out_shape=(
            pltpu.VMEM((8, 4, 2, 2, 2, rows, QUARTER), jnp.bfloat16),
            pltpu.VMEM((rows, width), jnp.float32),
            pltpu.VMEM((rows, width), jnp.float32),
        ),
        in_specs=[hbm] * 6,
        out_specs=(vmem, vmem, vmem),
        scratch_shapes=[
            pltpu.VMEM((2, rows, width // 2), jnp.bfloat16),
            pltpu.VMEM((2, rows, width // 2), jnp.bfloat16),
            pltpu.VMEM((2, rows, width // 2), jnp.float32),
            pltpu.VMEM((rows, width), jnp.float32),
            pltpu.VMEM((width // LANES, LANES), jnp.int32),
            pltpu.VMEM(kept.shape, jnp.int32),
            pltpu.VMEM((4, rows, QUARTER), jnp.float32),
            pltpu.VMEM((2, rows, QUARTER), jnp.float32),
            pltpu.VMEM((rows, QUARTER), jnp.float32),
            pltpu.VMEM((rows, QUARTER), jnp.float32),
            pltpu.VMEM((4, rows, QUARTER), jnp.float32),
            dma((9,)), dma((2,)), dma((2,)), dma((3,)), dma((3,)), dma((3,)), dma((3,)),
            dma, dma((number,)), dma, dma,
        ],
        compiler_params=pltpu.CompilerParams(
            collective_id=0, has_side_effects=True, vmem_limit_bytes=16 << 20
        ),
        name="exchange",
    )(
        stay(local_weights), stay(base), stay(error), stay(momentum),
        stay(signs.reshape(width // LANES, LANES)), stay(kept),
    )

    new_base, new_error, new_momentum = pl.pallas_call(
        store_kernel,
        out_shape=(
            jax.ShapeDtypeStruct((8, 4, 2, rows, width), jnp.bfloat16),
            jax.ShapeDtypeStruct((1, rows, width), jnp.float32),
            jax.ShapeDtypeStruct((rows, width), jnp.float32),
        ),
        in_specs=[vmem] * 3,
        out_specs=(hbm, hbm, hbm),
        scratch_shapes=[dma((34,))],
        compiler_params=pltpu.CompilerParams(vmem_limit_bytes=16 << 20),
        name="store",
    )(held(whole), held(fresh), held(dropped))
    return (new_base.reshape(64 * rows, width), new_error, new_momentum)


def solution(mesh):
    in_specs = (
        P("rep", "shard", None),
        P("shard", None),
        P("rep", "shard", None),
        P("shard", None),
        P(),
        P(),
    )
    out_specs = (P(), P("rep", "shard", None), P("shard", None))
    return jax.shard_map(shards, mesh=mesh, in_specs=in_specs, out_specs=out_specs, check_vma=False)
```

```python
import functools
import heapq

import jax
import jax.numpy as jnp
from jax import lax
from jax.experimental import pallas as pl
from jax.experimental.pallas import tpu as pltpu
from jax.sharding import PartitionSpec as P

MESH = pl.DeviceIdType.MESH
SIZES = {"x": 4, "y": 4, "z": 8}
AXES = ("x", "y", "z")
ROWS, QUARTER, LANES = 16, 2048, 128
PARTS = {"A": ("zxy", 0, 5), "B": ("zyx", 5, 6), "C": ("xyz", 11, 5)}
STRAIGHT = {("A", 1): (2,), ("B", 1): (3,), ("C", 1): (2,)}
CUT = {("A", 3): 3}
SINGLES = {"A": (1, 1), "B": (1, 1), "C": (0, 1)}
TILE_US, HOP_US, FAR_US, OP_US, LEAD_US = 0.092, 3.1, 0.65, 0.01, 0.8
OUTER = ("outer",)
OUTER_TILES = 32
FINISH_AFTER = 40


def messages():
    found, units = {}, {}

    def chain(part, stage, tag, axis, region, start):
        _, low, tiles = PARTS[part]
        straight = STRAIGHT.get((part, stage), ())
        arrived = {0: start}
        base = (part, stage) + tag
        half = SIZES[axis] // 2

        def add(name, step, far, place, first, last, after):
            spot = dict(region)
            spot[axis] = place
            unit = base + name
            whole = dict(spot)
            if place == half:
                unit = base + ("opposite",)
                if stage == 3 and tag[-1] == "one":
                    unit = (part, stage, "one", "opposite")
                    whole[PARTS[part][0][0]] = (0, 1)
            found[base + name] = dict(
                part=part, stage=stage, link=(axis, step), far=far, region=spot,
                tiles=(low + first, low + last), after=list(after), unit=unit,
            )
            units.setdefault(unit, (whole, (low, low + tiles), []))[2].append(base + name)
            if unit not in arrived.setdefault(place, []):
                arrived[place].append(unit)
            return [unit]

        if SIZES[axis] == 4:
            near = {step: add((step, 1), step, 1, step, 0, tiles, start) for step in (1, 3)}
            if 2 in straight:
                add((2, 2), 2, 2, 2, 0, tiles, start)
            else:
                cut = CUT.get((part, stage), tiles // 2)
                add((3, 2), 3, 1, 2, 0, cut, near[1])
                add((1, 2), 1, 1, 2, cut, tiles, near[3])
            return arrived
        for sign, first, last in ((1, 0, tiles // 2), (-1, tiles // 2, tiles)):
            behind = {0: start}
            for hop in range(1, half + 1):
                back = 0 if hop in straight else hop - 1
                span = (0, tiles) if hop < half else (first, last)
                place = -sign * hop if hop < half else half
                behind[hop] = add((sign, hop), sign * (hop - back), hop - back, place, *span, behind[back])
        return arrived

    for part, (order, _, _) in PARTS.items():
        one, two, three = order
        firsts = chain(part, 1, (), one, {one: 0, two: 0, three: 0}, [("own", part)])
        singles = [(off, {one: off, two: 0, three: 0}, names) for off, names in firsts.items()]
        together = [(9, {one: (0, 1), two: 0, three: 0}, [name for names in firsts.values() for name in names])]
        seconds = {}
        for off, region, names in singles if SINGLES[part][0] else together:
            for place, news in chain(part, 2, (off,), two, region, names).items():
                if place != 0:
                    seconds.setdefault(place, []).extend(news)
        for off, region, names in singles if SINGLES[part][1] else together:
            chain(part, 3, (off, "one"), three, region, names)
        for off, names in seconds.items():
            chain(part, 3, (off, "all"), three, {one: (0, 1), two: off, three: 0}, names)
    found[OUTER] = dict(
        part=None, stage=4, link=("y", 1), far=1, region={}, tiles=(0, OUTER_TILES),
        after=[("own", part) for part in PARTS], unit=OUTER,
    )
    units[OUTER] = ({}, None, [OUTER])
    return found, units


def count(region, tiles):
    wide = 1
    for axis, place in region.items():
        wide *= SIZES[axis] if isinstance(place, tuple) else 1
    return wide * (tiles[1] - tiles[0])


def forwards(found):
    groups = {}
    for message in found.values():
        part, stage, region = message["part"], message["stage"], message["region"]
        if part is None:
            continue
        order, low, tiles = PARTS[part]
        one, two, three = order
        key = (part, stage, region[two] if stage > 1 else 0, region[three] if stage > 2 else 0)
        entry = groups.setdefault(key, ({one: (0, 1), two: key[2], three: key[3]}, (low, low + tiles), set()))
        entry[2].add(message["unit"])
    for part in PARTS:
        groups[(part, 1, 0, 0)][2].add(("own", part))
    return list(groups.values())


def schedule(found, units, joined):
    users = {}
    for name, message in found.items():
        for before in message["after"]:
            users.setdefault(before, []).append(name)
    length = {name: count(message["region"], message["tiles"]) * TILE_US for name, message in found.items()}
    delay = {name: HOP_US + FAR_US * (message["far"] - 1) for name, message in found.items()}
    remaining = {}

    def path(name):
        if name not in remaining:
            after = [path(user) for user in users.get(found[name]["unit"], [])]
            remaining[name] = length[name] + delay[name] + max(after + [0.0])
        return remaining[name]

    def lanes(link):
        axis, step = link
        if axis == "z":
            return [((axis, 1 if step > 0 else -1), abs(step))]
        return [((axis, 1), 1), ((axis, 3), 1)] if step == 2 else [(link, 1)]

    needs = {name: len(message["after"]) for name, message in found.items()}
    flying = {unit: [len(names), 0.0] for unit, (_, _, names) in units.items()}
    cores = [set(names) for _, _, names in joined]
    arrivals = [(2 * (low + tiles) * TILE_US, -1, ("own", part)) for part, (_, low, tiles) in PARTS.items()]
    heapq.heapify(arrivals)
    queues, free, steps = {}, {}, []
    clock, ticket = 0.0, 0
    while arrivals or any(queues.values()):
        if arrivals and arrivals[0][0] <= clock:
            what = heapq.heappop(arrivals)[2]
            clock += OP_US
            steps.append(("wait", what))
            for user in users.get(what, []):
                needs[user] -= 1
                if needs[user] == 0:
                    ticket += 1
                    heapq.heappush(queues.setdefault(found[user]["link"], []), (-path(user), ticket, user))
            for names in cores:
                names.discard(what)
            clock += OP_US * sum(1 for names in cores if not names)
            cores = [names for names in cores if names]
            continue
        backlog = {
            link: max(free.get(lane, 0.0) for lane, _ in lanes(link)) for link, queue in queues.items() if queue
        }
        open_links = [(max(until - clock, 0.0), link) for link, until in backlog.items() if until - clock < LEAD_US]
        if open_links:
            _, _, name = heapq.heappop(queues[min(open_links)[1]])
            clock += OP_US
            steps.append(("send", name))
            end = 0.0
            for lane, times in lanes(found[name]["link"]):
                free[lane] = max(clock, free.get(lane, 0.0)) + length[name] * times
                end = max(end, free[lane])
            flight = flying[found[name]["unit"]]
            flight[0] -= 1
            flight[1] = max(flight[1], end + delay[name])
            if flight[0] == 0:
                ticket += 1
                heapq.heappush(arrivals, (flight[1], ticket, found[name]["unit"]))
            continue
        later = [until - LEAD_US + 1e-6 for until in backlog.values()]
        if arrivals:
            later.append(arrivals[0][0])
        clock = max(clock, min(later))
    return steps


def share(found, units, steps):
    at = {step: i for i, step in enumerate(steps)}
    links = {}
    for name, message in found.items():
        if message["part"] is not None:
            links.setdefault(message["link"], []).append((at["send", name], at["wait", message["unit"]]))

    def known(unit, name):
        axis, step = found[name]["link"]
        back = (axis, -step) if axis == "z" else (axis, step)
        over = at["wait", unit]
        return any(sent > over and taken < at["send", name] for sent, taken in links.get(back, []))

    spots, last = {}, []
    rest = [unit for unit in units if unit != OUTER]
    for unit in sorted(rest, key=lambda unit: min(at["send", name] for name in units[unit][2])):
        free = [i for i, old in enumerate(last) if all(known(old, name) for name in units[unit][2])]
        if free:
            spots[unit] = max(free, key=lambda i: at["wait", last[i]])
            last[spots[unit]] = unit
        else:
            spots[unit] = len(last)
            last.append(unit)
    return spots, len(last)


def parity_table(rows, columns):
    i = lax.broadcasted_iota(jnp.int32, (rows, columns), 0)
    j = lax.broadcasted_iota(jnp.int32, (rows, columns), 1)
    both = jnp.bitwise_and(jnp.bitwise_and(i, j), LANES - 1)
    for shift in (4, 2, 1):
        both = jnp.bitwise_xor(both, jnp.right_shift(both, shift))
    return (1 - 2 * jnp.bitwise_and(both, 1)).astype(jnp.bfloat16)


def rotate(tiles, table):
    number, rows, lanes = tiles.shape
    flat = tiles.reshape(number * rows, lanes)
    high = flat.astype(jnp.bfloat16)
    low = (flat - high.astype(jnp.float32)).astype(jnp.bfloat16)
    flat = jnp.dot(jnp.concatenate([high, low], axis=1), table, preferred_element_type=jnp.float32)
    near = 1
    while near < number:
        pairs = flat.reshape(number // (2 * near), 2, near * rows, lanes)
        flat = jnp.concatenate(
            [(pairs[:, 0] + pairs[:, 1])[:, None], (pairs[:, 0] - pairs[:, 1])[:, None]], axis=1
        )
        near *= 2
    return flat.reshape(number, rows, lanes)


def exchange_kernel(
    steps, found, units, joined, spots,
    lw_ref, base_ref, error_ref, momentum_ref, signs_ref, kept_ref,
    whole_ref, fresh_ref, dropped_ref,
    lw, base, error, momentum, signs, kept, part_sums, near, far, mine, outer,
    loads, near_recv, far_recv, outer_recv,
    all_send, message_recv, core_send, core_recv,
):
    rep, shard = lax.axis_index("rep"), lax.axis_index("shard")
    p, c = rep // 2, rep % 2
    x, y_high, z = (shard // 2) % 4, shard % 2, shard // 8
    block = base.shape[2]
    tiles_of_block = block // LANES

    def place_x(bits):
        return {0: x, 1: x + 1 - 2 * (x % 2), 2: (x + 2) % 4, 3: 3 - x}[bits]

    def place_y(bits):
        return (y_high if bits < 2 else 1 - y_high, p if bits % 2 == 0 else 1 - p)

    def place_z(step):
        return (z + step + SIZES["z"]) % SIZES["z"]

    def device(x_bits, y_bits, z_step, core):
        high, low = place_y(y_bits)
        return (low * 2 + core, place_z(z_step) * 8 + place_x(x_bits) * 2 + high)

    other_core = device(0, 0, 0, 1 - c)
    partner = device(0, 1, 0, c)

    def over(link):
        axis, step = link
        return device(step if axis == "x" else 0, step if axis == "y" else 0, step if axis == "z" else 0, c)

    copies = [pltpu.make_async_copy(signs_ref, signs, loads.at[0]), pltpu.make_async_copy(kept_ref, kept, loads.at[1])]
    for slot, b in enumerate((1 - p, p)):
        columns = pl.ds(pl.multiple_of(b * block, block), block)
        copies += [
            pltpu.make_async_copy(lw_ref.at[0, :, columns], lw.at[slot], loads.at[2 + 3 * slot]),
            pltpu.make_async_copy(base_ref.at[:, columns], base.at[slot], loads.at[3 + 3 * slot]),
            pltpu.make_async_copy(error_ref.at[0, :, columns], error.at[slot], loads.at[4 + 3 * slot]),
        ]
    copies.append(pltpu.make_async_copy(momentum_ref, momentum, loads.at[8]))
    for copy in copies:
        copy.start()

    barrier = pltpu.get_barrier_semaphore()
    peers = [over(link) for link in sorted({message["link"] for message in found.values()})] + [other_core]
    for target in peers:
        pl.semaphore_signal(barrier, inc=1, device_id=target, device_id_type=MESH)

    table = parity_table(2 * LANES, LANES)
    scale = 1.0 / 64.0

    def kept_mask(b):
        places = kept[pl.ds(b, 1), :]
        tile_hot = lax.broadcasted_iota(jnp.int32, (tiles_of_block, places.shape[1]), 0) == jnp.right_shift(places, 7)
        lane_hot = lax.broadcasted_iota(jnp.int32, (LANES, places.shape[1]), 0) == jnp.bitwise_and(places, LANES - 1)
        return lax.dot_general(
            tile_hot.astype(jnp.bfloat16), lane_hot.astype(jnp.bfloat16),
            (((1,), (1,)), ((), ())), preferred_element_type=jnp.float32,
        )[:, None, :]

    def sketch(slot, b, mask):
        for copy in copies[2 + 3 * slot:5 + 3 * slot]:
            copy.wait()
        compensated = (base[slot].astype(jnp.float32) - lw[slot].astype(jnp.float32)) + error[slot]
        comp = jnp.stack([compensated[:, t * LANES:(t + 1) * LANES] for t in range(tiles_of_block)])
        rows = pl.ds(pl.multiple_of(b * tiles_of_block, tiles_of_block), tiles_of_block)
        turn = signs[rows, :].astype(jnp.float32)[:, None, :]
        rotated = rotate(comp * turn, table) * scale
        back = rotate(jnp.where(mask > 0.5, rotated, 0.0), table) * (turn * scale)
        rest = comp - back
        half = tiles_of_block // 2
        for t in range(tiles_of_block):
            part_sums[2 * b + t // half, :, pl.ds((t % half) * LANES, LANES)] = back[t]
            dropped_ref[:, pl.ds(pl.multiple_of(b * block + t * LANES, LANES), LANES)] = rest[t]

    def remote(source, target, send, recv, where):
        return pltpu.make_async_remote_copy(
            src_ref=source, dst_ref=target, send_sem=send, recv_sem=recv, device_id=where, device_id_type=MESH
        )

    def at(region, tiles):
        def span(axis):
            i, cuts = region[axis]
            wide = SIZES[axis] // cuts
            return pl.ds(i * wide, wide)

        spot_x = span("x") if isinstance(region["x"], tuple) else place_x(region["x"])
        spot_z = span("z") if isinstance(region["z"], tuple) else place_z(region["z"])
        if isinstance(region["y"], tuple):
            high, low = pl.ds(region["y"][0], 2 // region["y"][1]), slice(None)
        else:
            high, low = place_y(region["y"])
        return whole_ref.at[spot_z, spot_x, high, low, c, :, pl.ds(tiles[0] * LANES, (tiles[1] - tiles[0]) * LANES)]

    to_far = remote(part_sums.at[2 * (1 - p) + 1 - c], near.at[0], all_send, near_recv.at[0], other_core)
    to_mine = remote(part_sums.at[2 * p + 1 - c], near.at[1], all_send, near_recv.at[1], other_core)
    copies[0].wait()
    copies[1].wait()
    first_mask = kept_mask(1 - p)
    sketch(0, 1 - p, first_mask)
    pl.semaphore_wait(barrier, len(peers))
    to_far.start()
    sketch(1, p, kept_mask(p))
    to_mine.start()
    to_far.wait_recv()
    pieces = {}
    for i, (part, (_, low, tiles)) in enumerate(PARTS.items()):
        columns = pl.ds(low * LANES, tiles * LANES)
        mine[:, columns] = part_sums[2 * (1 - p) + c, :, columns] + near[0, :, columns]
        pieces[part] = remote(mine.at[:, columns], far.at[:, columns], all_send, far_recv.at[i], partner)
        pieces[part].start()
    to_mine.wait_recv()
    copies[8].wait()

    mine_outer, their_outer = outer.at[2 * p + c], outer.at[2 * (1 - p) + c]
    outer_far = remote(mine_outer, mine_outer, all_send, outer_recv.at[0], partner)
    outer_near = remote(mine_outer, mine_outer, all_send, outer_recv.at[1], other_core)
    outer_last = remote(their_outer, their_outer, all_send, outer_recv.at[2], other_core)

    def send(name):
        message = found[name]
        axis, step = message["link"]
        region = dict(message["region"])
        region[axis] = region[axis] + step if axis == "z" else region[axis] ^ step
        place = at(region, message["tiles"])
        remote(
            place, place, all_send, message_recv.at[spots[message["unit"]]], over(message["link"]),
        ).start()

    def take(unit):
        region, tiles, _ = units[unit]
        place = at(region, tiles)
        remote(place, place, core_send, message_recv.at[spots[unit]], other_core).wait_recv()

    def own(part):
        _, low, tiles = PARTS[part]
        columns = pl.ds(low * LANES, tiles * LANES)
        pieces[part].wait_recv()
        total = (part_sums[2 * p + c, :, columns] + near[1, :, columns]) + far[:, columns]
        step = total * 0.25
        outer[2 * p + c, :, columns] = step
        wide = pl.ds(pl.multiple_of((2 * p + c) * QUARTER + low * LANES, LANES), tiles * LANES)
        fresh = 0.9 * momentum[:, wide] + step
        held = pl.ds(pl.multiple_of(c * QUARTER + low * LANES, LANES), tiles * LANES)
        lowered = base[1, :, held].astype(jnp.float32) - 0.7 * (step + 0.9 * fresh)
        whole_ref[z, x, y_high, p, c, :, columns] = lowered.astype(jnp.bfloat16)

    def finish():
        from_core = outer.at[2 * p + 1 - c]
        remote(from_core, from_core, all_send, outer_recv.at[1], other_core).wait_recv()
        from_core = outer.at[2 * (1 - p) + 1 - c]
        remote(from_core, from_core, all_send, outer_recv.at[2], other_core).wait_recv()
        for q in range(4):
            columns = pl.ds(q * QUARTER, QUARTER)
            fresh_ref[:, columns] = 0.9 * momentum[:, columns] + outer[q]

    waiting = [(set(group), region, tiles) for region, tiles, group in joined]
    outer_at = steps.index(("wait", OUTER))
    for i, (kind, what) in enumerate(steps):
        if i == outer_at + FINISH_AFTER:
            finish()
        if kind == "send":
            if what == OUTER:
                outer_far.start()
                outer_near.start()
            else:
                send(what)
            continue
        if what == OUTER:
            remote(their_outer, their_outer, all_send, outer_recv.at[0], partner).wait_recv()
            outer_last.start()
            continue
        if what[0] == "own":
            own(what[1])
        else:
            take(what)
        for group, _, _ in waiting:
            group.discard(what)
        for _, region, tiles in [entry for entry in waiting if not entry[0]]:
            place = at(region, tiles)
            remote(place, place, core_send, core_recv, other_core).start()
        waiting = [entry for entry in waiting if entry[0]]
    if outer_at + FINISH_AFTER >= len(steps):
        finish()

    for part, (order, low, tiles) in PARTS.items():
        columns = pl.ds(low * LANES, tiles * LANES)
        for stage in (1, 2, 3):
            ends = {axis: 1 for axis in AXES}
            for axis in order[:stage - 1]:
                ends[axis] = SIZES[axis]
            ends[order[stage - 1]] = SIZES[order[stage - 1]] - 1
            for high, low_y in {1: [(1, 1)], 3: [(1, 2), (1, 1)], 4: [(2, 2)]}[ends["y"]]:
                place = whole_ref.at[
                    pl.ds(0, ends["z"]), pl.ds(0, ends["x"]), pl.ds(0, high), pl.ds(0, low_y), c, :, columns
                ]
                remote(place, place, all_send, core_recv, other_core).wait_send()
    to_far.wait_send()
    to_mine.wait_send()
    for copy in list(pieces.values()) + [outer_far, outer_near, outer_last]:
        copy.wait_send()
    everything = whole_ref.at[:, :, :, :, c]
    remote(everything, everything, core_send, core_recv, other_core).wait_send()
    everything = whole_ref.at[:, :, :, :, 1 - c]
    remote(everything, everything, core_send, core_recv, other_core).wait_recv()


def store_kernel(whole_ref, fresh_ref, dropped_ref, base_out, error_out, momentum_out, sems):
    copies = [
        pltpu.make_async_copy(fresh_ref, momentum_out, sems.at[0]),
        pltpu.make_async_copy(dropped_ref, error_out.at[0], sems.at[1]),
    ]
    for z in range(whole_ref.shape[0]):
        for low in range(2):
            for core in range(2):
                copies.append(pltpu.make_async_copy(
                    whole_ref.at[z, :, :, low, core],
                    base_out.at[z, :, :, :, pl.ds((2 * low + core) * QUARTER, QUARTER)],
                    sems.at[len(copies)],
                ))
    for copy in copies:
        copy.start()
    for copy in copies:
        copy.wait()


def shards(local_weights, base, error, momentum, signs, kept):
    rows, width = base.shape
    vmem = pl.BlockSpec(memory_space=pltpu.VMEM)
    hbm = pl.BlockSpec(memory_space=pl.ANY)
    held = lambda array: pltpu.with_memory_space_constraint(array, pltpu.VMEM)
    stay = lambda array: pltpu.with_memory_space_constraint(array, pltpu.HBM)
    found, units = messages()
    joined = forwards(found)
    steps = schedule(found, units, joined)
    spots, number = share(found, units, steps)
    dma = pltpu.SemaphoreType.DMA
    whole, fresh, dropped = pl.pallas_call(
        functools.partial(exchange_kernel, steps, found, units, joined, spots),
        out_shape=(
            pltpu.VMEM((8, 4, 2, 2, 2, rows, QUARTER), jnp.bfloat16),
            pltpu.VMEM((rows, width), jnp.float32),
            pltpu.VMEM((rows, width), jnp.float32),
        ),
        in_specs=[hbm] * 6,
        out_specs=(vmem, vmem, vmem),
        scratch_shapes=[
            pltpu.VMEM((2, rows, width // 2), jnp.bfloat16),
            pltpu.VMEM((2, rows, width // 2), jnp.bfloat16),
            pltpu.VMEM((2, rows, width // 2), jnp.float32),
            pltpu.VMEM((rows, width), jnp.float32),
            pltpu.VMEM((width // LANES, LANES), jnp.int32),
            pltpu.VMEM(kept.shape, jnp.int32),
            pltpu.VMEM((4, rows, QUARTER), jnp.float32),
            pltpu.VMEM((2, rows, QUARTER), jnp.float32),
            pltpu.VMEM((rows, QUARTER), jnp.float32),
            pltpu.VMEM((rows, QUARTER), jnp.float32),
            pltpu.VMEM((4, rows, QUARTER), jnp.float32),
            dma((9,)), dma((2,)), dma((3,)), dma((3,)), dma, dma((number,)), dma, dma,
        ],
        compiler_params=pltpu.CompilerParams(
            collective_id=0, has_side_effects=True, vmem_limit_bytes=16 << 20
        ),
        name="exchange",
    )(
        stay(local_weights), stay(base), stay(error), stay(momentum),
        stay(signs.reshape(width // LANES, LANES)), stay(kept),
    )

    new_base, new_error, new_momentum = pl.pallas_call(
        store_kernel,
        out_shape=(
            jax.ShapeDtypeStruct((8, 4, 2, rows, width), jnp.bfloat16),
            jax.ShapeDtypeStruct((1, rows, width), jnp.float32),
            jax.ShapeDtypeStruct((rows, width), jnp.float32),
        ),
        in_specs=[vmem] * 3,
        out_specs=(hbm, hbm, hbm),
        scratch_shapes=[dma((34,))],
        compiler_params=pltpu.CompilerParams(vmem_limit_bytes=16 << 20),
        name="store",
    )(held(whole), held(fresh), held(dropped))
    return (new_base.reshape(64 * rows, width), new_error, new_momentum)


def solution(mesh):
    in_specs = (
        P("rep", "shard", None),
        P("shard", None),
        P("rep", "shard", None),
        P("shard", None),
        P(),
        P(),
    )
    out_specs = (P(), P("rep", "shard", None), P("shard", None))
    return jax.shard_map(shards, mesh=mesh, in_specs=in_specs, out_specs=out_specs, check_vma=False)
```

```python
import functools
import heapq

import jax
import jax.numpy as jnp
from jax import lax
from jax.experimental import pallas as pl
from jax.experimental.pallas import tpu as pltpu
from jax.sharding import PartitionSpec as P

MESH = pl.DeviceIdType.MESH
SIZES = {"x": 4, "y": 4, "z": 8}
AXES = ("x", "y", "z")
ROWS, QUARTER, LANES = 16, 2048, 128
PARTS = {"A": ("zxy", 0, 5), "B": ("zyx", 5, 6), "C": ("xyz", 11, 5)}
STRAIGHT = {("A", 1): (2,), ("B", 1): (3,), ("C", 1): (2,)}
CUT = {("A", 3): 3}
SINGLES = {"A": (1, 1), "B": (1, 1), "C": (0, 1)}
TILE_US, HOP_US, FAR_US, OP_US, LEAD_US = 0.092, 3.1, 0.65, 0.01, 0.8
OUTER = ("outer",)
OUTER_TILES = 32
FINISH_AFTER = 40


def messages():
    found, units = {}, {}

    def chain(part, stage, tag, axis, region, start):
        _, low, tiles = PARTS[part]
        straight = STRAIGHT.get((part, stage), ())
        arrived = {0: start}
        base = (part, stage) + tag
        half = SIZES[axis] // 2

        def add(name, step, far, place, first, last, after):
            spot = dict(region)
            spot[axis] = place
            unit = base + name
            whole = dict(spot)
            if place == half:
                unit = base + ("opposite",)
                if stage == 3 and tag[-1] == "one":
                    unit = (part, stage, "one", "opposite")
                    whole[PARTS[part][0][0]] = (0, 1)
            found[base + name] = dict(
                part=part, stage=stage, link=(axis, step), far=far, region=spot,
                tiles=(low + first, low + last), after=list(after), unit=unit,
            )
            units.setdefault(unit, (whole, (low, low + tiles), []))[2].append(base + name)
            if unit not in arrived.setdefault(place, []):
                arrived[place].append(unit)
            return [unit]

        if SIZES[axis] == 4:
            near = {step: add((step, 1), step, 1, step, 0, tiles, start) for step in (1, 3)}
            if 2 in straight:
                add((2, 2), 2, 2, 2, 0, tiles, start)
            else:
                cut = CUT.get((part, stage), tiles // 2)
                add((3, 2), 3, 1, 2, 0, cut, near[1])
                add((1, 2), 1, 1, 2, cut, tiles, near[3])
            return arrived
        for sign, first, last in ((1, 0, tiles // 2), (-1, tiles // 2, tiles)):
            behind = {0: start}
            for hop in range(1, half + 1):
                back = 0 if hop in straight else hop - 1
                span = (0, tiles) if hop < half else (first, last)
                place = -sign * hop if hop < half else half
                behind[hop] = add((sign, hop), sign * (hop - back), hop - back, place, *span, behind[back])
        return arrived

    for part, (order, _, _) in PARTS.items():
        one, two, three = order
        firsts = chain(part, 1, (), one, {one: 0, two: 0, three: 0}, [("own", part)])
        singles = [(off, {one: off, two: 0, three: 0}, names) for off, names in firsts.items()]
        together = [(9, {one: (0, 1), two: 0, three: 0}, [name for names in firsts.values() for name in names])]
        seconds = {}
        for off, region, names in singles if SINGLES[part][0] else together:
            for place, news in chain(part, 2, (off,), two, region, names).items():
                if place != 0:
                    seconds.setdefault(place, []).extend(news)
        for off, region, names in singles if SINGLES[part][1] else together:
            chain(part, 3, (off, "one"), three, region, names)
        for off, names in seconds.items():
            chain(part, 3, (off, "all"), three, {one: (0, 1), two: off, three: 0}, names)
    found[OUTER] = dict(
        part=None, stage=4, link=("y", 1), far=1, region={}, tiles=(0, OUTER_TILES),
        after=[("own", part) for part in PARTS], unit=OUTER,
    )
    units[OUTER] = ({}, None, [OUTER])
    return found, units


def count(region, tiles):
    wide = 1
    for axis, place in region.items():
        wide *= SIZES[axis] if isinstance(place, tuple) else 1
    return wide * (tiles[1] - tiles[0])


def forwards(found):
    groups = {}
    for message in found.values():
        part, stage, region = message["part"], message["stage"], message["region"]
        if part is None:
            continue
        order, low, tiles = PARTS[part]
        one, two, three = order
        key = (part, stage, region[two] if stage > 1 else 0, region[three] if stage > 2 else 0)
        entry = groups.setdefault(key, ({one: (0, 1), two: key[2], three: key[3]}, (low, low + tiles), set()))
        entry[2].add(message["unit"])
    for part in PARTS:
        groups[(part, 1, 0, 0)][2].add(("own", part))
    return list(groups.values())


def schedule(found, units, joined):
    users = {}
    for name, message in found.items():
        for before in message["after"]:
            users.setdefault(before, []).append(name)
    length = {name: count(message["region"], message["tiles"]) * TILE_US for name, message in found.items()}
    delay = {name: HOP_US + FAR_US * (message["far"] - 1) for name, message in found.items()}
    remaining = {}

    def path(name):
        if name not in remaining:
            after = [path(user) for user in users.get(found[name]["unit"], [])]
            remaining[name] = length[name] + delay[name] + max(after + [0.0])
        return remaining[name]

    def lanes(link):
        axis, step = link
        if axis == "z":
            return [((axis, 1 if step > 0 else -1), abs(step))]
        return [((axis, 1), 1), ((axis, 3), 1)] if step == 2 else [(link, 1)]

    needs = {name: len(message["after"]) for name, message in found.items()}
    flying = {unit: [len(names), 0.0] for unit, (_, _, names) in units.items()}
    cores = [set(names) for _, _, names in joined]
    arrivals = [(2 * (low + tiles) * TILE_US, -1, ("own", part)) for part, (_, low, tiles) in PARTS.items()]
    heapq.heapify(arrivals)
    queues, free, steps = {}, {}, []
    clock, ticket = 0.0, 0
    while arrivals or any(queues.values()):
        if arrivals and arrivals[0][0] <= clock:
            what = heapq.heappop(arrivals)[2]
            clock += OP_US
            steps.append(("wait", what))
            for user in users.get(what, []):
                needs[user] -= 1
                if needs[user] == 0:
                    ticket += 1
                    heapq.heappush(queues.setdefault(found[user]["link"], []), (-path(user), ticket, user))
            for names in cores:
                names.discard(what)
            clock += OP_US * sum(1 for names in cores if not names)
            cores = [names for names in cores if names]
            continue
        backlog = {
            link: max(free.get(lane, 0.0) for lane, _ in lanes(link)) for link, queue in queues.items() if queue
        }
        open_links = [(max(until - clock, 0.0), link) for link, until in backlog.items() if until - clock < LEAD_US]
        if open_links:
            _, _, name = heapq.heappop(queues[min(open_links)[1]])
            clock += OP_US
            steps.append(("send", name))
            end = 0.0
            for lane, times in lanes(found[name]["link"]):
                free[lane] = max(clock, free.get(lane, 0.0)) + length[name] * times
                end = max(end, free[lane])
            flight = flying[found[name]["unit"]]
            flight[0] -= 1
            flight[1] = max(flight[1], end + delay[name])
            if flight[0] == 0:
                ticket += 1
                heapq.heappush(arrivals, (flight[1], ticket, found[name]["unit"]))
            continue
        later = [until - LEAD_US + 1e-6 for until in backlog.values()]
        if arrivals:
            later.append(arrivals[0][0])
        clock = max(clock, min(later))
    return steps


def share(found, units, steps):
    at = {step: i for i, step in enumerate(steps)}
    links = {}
    for name, message in found.items():
        if message["part"] is not None:
            links.setdefault(message["link"], []).append((at["send", name], at["wait", message["unit"]]))

    def known(unit, name):
        axis, step = found[name]["link"]
        back = (axis, -step) if axis == "z" else (axis, step)
        over = at["wait", unit]
        return any(sent > over and taken < at["send", name] for sent, taken in links.get(back, []))

    spots, last = {}, []
    rest = [unit for unit in units if unit != OUTER]
    for unit in sorted(rest, key=lambda unit: min(at["send", name] for name in units[unit][2])):
        free = [i for i, old in enumerate(last) if all(known(old, name) for name in units[unit][2])]
        if free:
            spots[unit] = max(free, key=lambda i: at["wait", last[i]])
            last[spots[unit]] = unit
        else:
            spots[unit] = len(last)
            last.append(unit)
    return spots, len(last)


def parity_table(rows, columns):
    i = lax.broadcasted_iota(jnp.int32, (rows, columns), 0)
    j = lax.broadcasted_iota(jnp.int32, (rows, columns), 1)
    both = jnp.bitwise_and(jnp.bitwise_and(i, j), LANES - 1)
    for shift in (4, 2, 1):
        both = jnp.bitwise_xor(both, jnp.right_shift(both, shift))
    return (1 - 2 * jnp.bitwise_and(both, 1)).astype(jnp.bfloat16)


def rotate(tiles, table):
    number, rows, lanes = tiles.shape
    flat = tiles.reshape(number * rows, lanes)
    high = flat.astype(jnp.bfloat16)
    low = (flat - high.astype(jnp.float32)).astype(jnp.bfloat16)
    flat = jnp.dot(jnp.concatenate([high, low], axis=1), table, preferred_element_type=jnp.float32)
    near = 1
    while near < number:
        pairs = flat.reshape(number // (2 * near), 2, near * rows, lanes)
        flat = jnp.concatenate(
            [(pairs[:, 0] + pairs[:, 1])[:, None], (pairs[:, 0] - pairs[:, 1])[:, None]], axis=1
        )
        near *= 2
    return flat.reshape(number, rows, lanes)


def exchange_kernel(
    steps, found, units, joined, spots,
    lw_ref, base_ref, error_ref, momentum_ref, signs_ref, kept_ref,
    whole_ref, fresh_ref, dropped_ref,
    lw, base, error, momentum, signs, kept, part_sums, near, far, mine, outer,
    loads, near_recv, far_recv, outer_recv,
    all_send, message_recv, core_send, core_recv,
):
    rep, shard = lax.axis_index("rep"), lax.axis_index("shard")
    p, c = rep // 2, rep % 2
    x, y_high, z = (shard // 2) % 4, shard % 2, shard // 8
    block = base.shape[2]
    tiles_of_block = block // LANES

    def place_x(bits):
        return {0: x, 1: x + 1 - 2 * (x % 2), 2: (x + 2) % 4, 3: 3 - x}[bits]

    def place_y(bits):
        return (y_high if bits < 2 else 1 - y_high, p if bits % 2 == 0 else 1 - p)

    def place_z(step):
        return (z + step + SIZES["z"]) % SIZES["z"]

    def device(x_bits, y_bits, z_step, core):
        high, low = place_y(y_bits)
        return (low * 2 + core, place_z(z_step) * 8 + place_x(x_bits) * 2 + high)

    other_core = device(0, 0, 0, 1 - c)
    partner = device(0, 1, 0, c)

    def over(link):
        axis, step = link
        return device(step if axis == "x" else 0, step if axis == "y" else 0, step if axis == "z" else 0, c)

    copies = [pltpu.make_async_copy(signs_ref, signs, loads.at[0]), pltpu.make_async_copy(kept_ref, kept, loads.at[1])]
    for slot, b in enumerate((1 - p, p)):
        columns = pl.ds(pl.multiple_of(b * block, block), block)
        copies += [
            pltpu.make_async_copy(lw_ref.at[0, :, columns], lw.at[slot], loads.at[2 + 3 * slot]),
            pltpu.make_async_copy(base_ref.at[:, columns], base.at[slot], loads.at[3 + 3 * slot]),
            pltpu.make_async_copy(error_ref.at[0, :, columns], error.at[slot], loads.at[4 + 3 * slot]),
        ]
    copies.append(pltpu.make_async_copy(momentum_ref, momentum, loads.at[8]))
    for copy in copies:
        copy.start()

    barrier = pltpu.get_barrier_semaphore()
    peers = [over(link) for link in sorted({message["link"] for message in found.values()})] + [other_core]
    for target in peers:
        pl.semaphore_signal(barrier, inc=1, device_id=target, device_id_type=MESH)

    table = parity_table(2 * LANES, LANES)
    scale = 1.0 / 64.0

    def kept_mask(b):
        places = kept[pl.ds(b, 1), :]
        tile_hot = lax.broadcasted_iota(jnp.int32, (tiles_of_block, places.shape[1]), 0) == jnp.right_shift(places, 7)
        lane_hot = lax.broadcasted_iota(jnp.int32, (LANES, places.shape[1]), 0) == jnp.bitwise_and(places, LANES - 1)
        return lax.dot_general(
            tile_hot.astype(jnp.bfloat16), lane_hot.astype(jnp.bfloat16),
            (((1,), (1,)), ((), ())), preferred_element_type=jnp.float32,
        )[:, None, :]

    def sketch(slot, b, mask):
        for copy in copies[2 + 3 * slot:5 + 3 * slot]:
            copy.wait()
        compensated = (base[slot].astype(jnp.float32) - lw[slot].astype(jnp.float32)) + error[slot]
        comp = jnp.stack([compensated[:, t * LANES:(t + 1) * LANES] for t in range(tiles_of_block)])
        rows = pl.ds(pl.multiple_of(b * tiles_of_block, tiles_of_block), tiles_of_block)
        turn = signs[rows, :].astype(jnp.float32)[:, None, :]
        rotated = rotate(comp * turn, table) * scale
        back = rotate(jnp.where(mask > 0.5, rotated, 0.0), table) * (turn * scale)
        half = tiles_of_block // 2
        for t in range(tiles_of_block):
            part_sums[2 * b + t // half, :, pl.ds((t % half) * LANES, LANES)] = back[t]
        return comp - back

    def keep_rest(b, rest):
        for t in range(tiles_of_block):
            dropped_ref[:, pl.ds(pl.multiple_of(b * block + t * LANES, LANES), LANES)] = rest[t]

    def remote(source, target, send, recv, where):
        return pltpu.make_async_remote_copy(
            src_ref=source, dst_ref=target, send_sem=send, recv_sem=recv, device_id=where, device_id_type=MESH
        )

    def at(region, tiles):
        def span(axis):
            i, cuts = region[axis]
            wide = SIZES[axis] // cuts
            return pl.ds(i * wide, wide)

        spot_x = span("x") if isinstance(region["x"], tuple) else place_x(region["x"])
        spot_z = span("z") if isinstance(region["z"], tuple) else place_z(region["z"])
        if isinstance(region["y"], tuple):
            high, low = pl.ds(region["y"][0], 2 // region["y"][1]), slice(None)
        else:
            high, low = place_y(region["y"])
        return whole_ref.at[spot_z, spot_x, high, low, c, :, pl.ds(tiles[0] * LANES, (tiles[1] - tiles[0]) * LANES)]

    first = next(iter(PARTS.values()))[2] * LANES
    to_far = []
    for i, columns in enumerate((pl.ds(0, first), pl.ds(first, QUARTER - first))):
        to_far.append(remote(
            part_sums.at[2 * (1 - p) + 1 - c, :, columns], near.at[0, :, columns], all_send, near_recv.at[i], other_core
        ))
    to_mine = remote(part_sums.at[2 * p + 1 - c], near.at[1], all_send, near_recv.at[2], other_core)
    copies[0].wait()
    copies[1].wait()
    first_mask = kept_mask(1 - p)
    rest = sketch(0, 1 - p, first_mask)
    pl.semaphore_wait(barrier, len(peers))
    for copy in to_far:
        copy.start()
    keep_rest(1 - p, rest)
    rest = sketch(1, p, kept_mask(p))
    to_mine.start()
    pieces = {}
    for i, (part, (_, low, tiles)) in enumerate(PARTS.items()):
        columns = pl.ds(low * LANES, tiles * LANES)
        if i < 2:
            to_far[i].wait_recv()
        mine[:, columns] = part_sums[2 * (1 - p) + c, :, columns] + near[0, :, columns]
        pieces[part] = remote(mine.at[:, columns], far.at[:, columns], all_send, far_recv.at[i], partner)
        pieces[part].start()
    keep_rest(p, rest)
    to_mine.wait_recv()
    copies[8].wait()

    mine_outer, their_outer = outer.at[2 * p + c], outer.at[2 * (1 - p) + c]
    outer_far = remote(mine_outer, mine_outer, all_send, outer_recv.at[0], partner)
    outer_near = remote(mine_outer, mine_outer, all_send, outer_recv.at[1], other_core)
    outer_last = remote(their_outer, their_outer, all_send, outer_recv.at[2], other_core)

    def send(name):
        message = found[name]
        axis, step = message["link"]
        region = dict(message["region"])
        region[axis] = region[axis] + step if axis == "z" else region[axis] ^ step
        place = at(region, message["tiles"])
        remote(
            place, place, all_send, message_recv.at[spots[message["unit"]]], over(message["link"]),
        ).start()

    def take(unit):
        region, tiles, _ = units[unit]
        place = at(region, tiles)
        remote(place, place, core_send, message_recv.at[spots[unit]], other_core).wait_recv()

    def own(part):
        _, low, tiles = PARTS[part]
        columns = pl.ds(low * LANES, tiles * LANES)
        pieces[part].wait_recv()
        total = (part_sums[2 * p + c, :, columns] + near[1, :, columns]) + far[:, columns]
        step = total * 0.25
        outer[2 * p + c, :, columns] = step
        wide = pl.ds(pl.multiple_of((2 * p + c) * QUARTER + low * LANES, LANES), tiles * LANES)
        fresh = 0.9 * momentum[:, wide] + step
        held = pl.ds(pl.multiple_of(c * QUARTER + low * LANES, LANES), tiles * LANES)
        lowered = base[1, :, held].astype(jnp.float32) - 0.7 * (step + 0.9 * fresh)
        whole_ref[z, x, y_high, p, c, :, columns] = lowered.astype(jnp.bfloat16)

    def finish():
        from_core = outer.at[2 * p + 1 - c]
        remote(from_core, from_core, all_send, outer_recv.at[1], other_core).wait_recv()
        from_core = outer.at[2 * (1 - p) + 1 - c]
        remote(from_core, from_core, all_send, outer_recv.at[2], other_core).wait_recv()
        for q in range(4):
            columns = pl.ds(q * QUARTER, QUARTER)
            fresh_ref[:, columns] = 0.9 * momentum[:, columns] + outer[q]

    waiting = [(set(group), region, tiles) for region, tiles, group in joined]
    outer_at = steps.index(("wait", OUTER))
    for i, (kind, what) in enumerate(steps):
        if i == outer_at + FINISH_AFTER:
            finish()
        if kind == "send":
            if what == OUTER:
                outer_far.start()
                outer_near.start()
            else:
                send(what)
            continue
        if what == OUTER:
            remote(their_outer, their_outer, all_send, outer_recv.at[0], partner).wait_recv()
            outer_last.start()
            continue
        if what[0] == "own":
            own(what[1])
        else:
            take(what)
        for group, _, _ in waiting:
            group.discard(what)
        for _, region, tiles in [entry for entry in waiting if not entry[0]]:
            place = at(region, tiles)
            remote(place, place, core_send, core_recv, other_core).start()
        waiting = [entry for entry in waiting if entry[0]]
    if outer_at + FINISH_AFTER >= len(steps):
        finish()

    for part, (order, low, tiles) in PARTS.items():
        columns = pl.ds(low * LANES, tiles * LANES)
        for stage in (1, 2, 3):
            ends = {axis: 1 for axis in AXES}
            for axis in order[:stage - 1]:
                ends[axis] = SIZES[axis]
            ends[order[stage - 1]] = SIZES[order[stage - 1]] - 1
            for high, low_y in {1: [(1, 1)], 3: [(1, 2), (1, 1)], 4: [(2, 2)]}[ends["y"]]:
                place = whole_ref.at[
                    pl.ds(0, ends["z"]), pl.ds(0, ends["x"]), pl.ds(0, high), pl.ds(0, low_y), c, :, columns
                ]
                remote(place, place, all_send, core_recv, other_core).wait_send()
    for copy in to_far + [to_mine] + list(pieces.values()) + [outer_far, outer_near, outer_last]:
        copy.wait_send()
    everything = whole_ref.at[:, :, :, :, c]
    remote(everything, everything, core_send, core_recv, other_core).wait_send()
    everything = whole_ref.at[:, :, :, :, 1 - c]
    remote(everything, everything, core_send, core_recv, other_core).wait_recv()


def store_kernel(whole_ref, fresh_ref, dropped_ref, base_out, error_out, momentum_out, sems):
    copies = [
        pltpu.make_async_copy(fresh_ref, momentum_out, sems.at[0]),
        pltpu.make_async_copy(dropped_ref, error_out.at[0], sems.at[1]),
    ]
    for z in range(whole_ref.shape[0]):
        for low in range(2):
            for core in range(2):
                copies.append(pltpu.make_async_copy(
                    whole_ref.at[z, :, :, low, core],
                    base_out.at[z, :, :, :, pl.ds((2 * low + core) * QUARTER, QUARTER)],
                    sems.at[len(copies)],
                ))
    for copy in copies:
        copy.start()
    for copy in copies:
        copy.wait()


def shards(local_weights, base, error, momentum, signs, kept):
    rows, width = base.shape
    vmem = pl.BlockSpec(memory_space=pltpu.VMEM)
    hbm = pl.BlockSpec(memory_space=pl.ANY)
    held = lambda array: pltpu.with_memory_space_constraint(array, pltpu.VMEM)
    stay = lambda array: pltpu.with_memory_space_constraint(array, pltpu.HBM)
    found, units = messages()
    joined = forwards(found)
    steps = schedule(found, units, joined)
    spots, number = share(found, units, steps)
    dma = pltpu.SemaphoreType.DMA
    whole, fresh, dropped = pl.pallas_call(
        functools.partial(exchange_kernel, steps, found, units, joined, spots),
        out_shape=(
            pltpu.VMEM((8, 4, 2, 2, 2, rows, QUARTER), jnp.bfloat16),
            pltpu.VMEM((rows, width), jnp.float32),
            pltpu.VMEM((rows, width), jnp.float32),
        ),
        in_specs=[hbm] * 6,
        out_specs=(vmem, vmem, vmem),
        scratch_shapes=[
            pltpu.VMEM((2, rows, width // 2), jnp.bfloat16),
            pltpu.VMEM((2, rows, width // 2), jnp.bfloat16),
            pltpu.VMEM((2, rows, width // 2), jnp.float32),
            pltpu.VMEM((rows, width), jnp.float32),
            pltpu.VMEM((width // LANES, LANES), jnp.int32),
            pltpu.VMEM(kept.shape, jnp.int32),
            pltpu.VMEM((4, rows, QUARTER), jnp.float32),
            pltpu.VMEM((2, rows, QUARTER), jnp.float32),
            pltpu.VMEM((rows, QUARTER), jnp.float32),
            pltpu.VMEM((rows, QUARTER), jnp.float32),
            pltpu.VMEM((4, rows, QUARTER), jnp.float32),
            dma((9,)), dma((3,)), dma((3,)), dma((3,)), dma, dma((number,)), dma, dma,
        ],
        compiler_params=pltpu.CompilerParams(
            collective_id=0, has_side_effects=True, vmem_limit_bytes=16 << 20
        ),
        name="exchange",
    )(
        stay(local_weights), stay(base), stay(error), stay(momentum),
        stay(signs.reshape(width // LANES, LANES)), stay(kept),
    )

    new_base, new_error, new_momentum = pl.pallas_call(
        store_kernel,
        out_shape=(
            jax.ShapeDtypeStruct((8, 4, 2, rows, width), jnp.bfloat16),
            jax.ShapeDtypeStruct((1, rows, width), jnp.float32),
            jax.ShapeDtypeStruct((rows, width), jnp.float32),
        ),
        in_specs=[vmem] * 3,
        out_specs=(hbm, hbm, hbm),
        scratch_shapes=[dma((34,))],
        compiler_params=pltpu.CompilerParams(vmem_limit_bytes=16 << 20),
        name="store",
    )(held(whole), held(fresh), held(dropped))
    return (new_base.reshape(64 * rows, width), new_error, new_momentum)


def solution(mesh):
    in_specs = (
        P("rep", "shard", None),
        P("shard", None),
        P("rep", "shard", None),
        P("shard", None),
        P(),
        P(),
    )
    out_specs = (P(), P("rep", "shard", None), P("shard", None))
    return jax.shard_map(shards, mesh=mesh, in_specs=in_specs, out_specs=out_specs, check_vma=False)
```

```python
import functools
import heapq

import jax
import jax.numpy as jnp
from jax import lax
from jax.experimental import pallas as pl
from jax.experimental.pallas import tpu as pltpu
from jax.sharding import PartitionSpec as P

MESH = pl.DeviceIdType.MESH
SIZES = {"x": 4, "y": 4, "z": 8}
AXES = ("x", "y", "z")
ROWS, QUARTER, LANES = 16, 2048, 128
PARTS = {"A": ("zxy", 0, 5), "B": ("zyx", 5, 6), "C": ("xyz", 11, 5)}
STRAIGHT = {("A", 1): (2,), ("B", 1): (3,), ("C", 1): (2,)}
CUT = {("A", 3): 3}
SINGLES = {"A": (1, 1), "B": (1, 1), "C": (0, 1)}
TILE_US, HOP_US, FAR_US, OP_US, LEAD_US = 0.092, 3.1, 0.65, 0.01, 0.8
OUTER = ("outer",)
OUTER_TILES = 32
FINISH_AFTER = 40


def messages():
    found, units = {}, {}

    def chain(part, stage, tag, axis, region, start):
        _, low, tiles = PARTS[part]
        straight = STRAIGHT.get((part, stage), ())
        arrived = {0: start}
        base = (part, stage) + tag
        half = SIZES[axis] // 2

        def add(name, step, far, place, first, last, after):
            spot = dict(region)
            spot[axis] = place
            unit = base + name
            whole = dict(spot)
            if place == half:
                unit = base + ("opposite",)
                if stage == 3 and tag[-1] == "one":
                    unit = (part, stage, "one", "opposite")
                    whole[PARTS[part][0][0]] = (0, 1)
            found[base + name] = dict(
                part=part, stage=stage, link=(axis, step), far=far, region=spot,
                tiles=(low + first, low + last), after=list(after), unit=unit,
            )
            units.setdefault(unit, (whole, (low, low + tiles), []))[2].append(base + name)
            if unit not in arrived.setdefault(place, []):
                arrived[place].append(unit)
            return [unit]

        if SIZES[axis] == 4:
            near = {step: add((step, 1), step, 1, step, 0, tiles, start) for step in (1, 3)}
            if 2 in straight:
                add((2, 2), 2, 2, 2, 0, tiles, start)
            else:
                cut = CUT.get((part, stage), tiles // 2)
                add((3, 2), 3, 1, 2, 0, cut, near[1])
                add((1, 2), 1, 1, 2, cut, tiles, near[3])
            return arrived
        for sign, first, last in ((1, 0, tiles // 2), (-1, tiles // 2, tiles)):
            behind = {0: start}
            for hop in range(1, half + 1):
                back = 0 if hop in straight else hop - 1
                span = (0, tiles) if hop < half else (first, last)
                place = -sign * hop if hop < half else half
                behind[hop] = add((sign, hop), sign * (hop - back), hop - back, place, *span, behind[back])
        return arrived

    for part, (order, _, _) in PARTS.items():
        one, two, three = order
        firsts = chain(part, 1, (), one, {one: 0, two: 0, three: 0}, [("own", part)])
        singles = [(off, {one: off, two: 0, three: 0}, names) for off, names in firsts.items()]
        together = [(9, {one: (0, 1), two: 0, three: 0}, [name for names in firsts.values() for name in names])]
        seconds = {}
        for off, region, names in singles if SINGLES[part][0] else together:
            for place, news in chain(part, 2, (off,), two, region, names).items():
                if place != 0:
                    seconds.setdefault(place, []).extend(news)
        for off, region, names in singles if SINGLES[part][1] else together:
            chain(part, 3, (off, "one"), three, region, names)
        for off, names in seconds.items():
            chain(part, 3, (off, "all"), three, {one: (0, 1), two: off, three: 0}, names)
    found[OUTER] = dict(
        part=None, stage=4, link=("y", 1), far=1, region={}, tiles=(0, OUTER_TILES),
        after=[("own", part) for part in PARTS], unit=OUTER,
    )
    units[OUTER] = ({}, None, [OUTER])
    return found, units


def count(region, tiles):
    wide = 1
    for axis, place in region.items():
        wide *= SIZES[axis] if isinstance(place, tuple) else 1
    return wide * (tiles[1] - tiles[0])


def forwards(found):
    groups = {}
    for message in found.values():
        part, stage, region = message["part"], message["stage"], message["region"]
        if part is None:
            continue
        order, low, tiles = PARTS[part]
        one, two, three = order
        key = (part, stage, region[two] if stage > 1 else 0, region[three] if stage > 2 else 0)
        entry = groups.setdefault(key, ({one: (0, 1), two: key[2], three: key[3]}, (low, low + tiles), set()))
        entry[2].add(message["unit"])
    for part in PARTS:
        groups[(part, 1, 0, 0)][2].add(("own", part))
    return list(groups.values())


def schedule(found, units, joined):
    users = {}
    for name, message in found.items():
        for before in message["after"]:
            users.setdefault(before, []).append(name)
    length = {name: count(message["region"], message["tiles"]) * TILE_US for name, message in found.items()}
    delay = {name: HOP_US + FAR_US * (message["far"] - 1) for name, message in found.items()}
    remaining = {}

    def path(name):
        if name not in remaining:
            after = [path(user) for user in users.get(found[name]["unit"], [])]
            remaining[name] = length[name] + delay[name] + max(after + [0.0])
        return remaining[name]

    def lanes(link):
        axis, step = link
        if axis == "z":
            return [((axis, 1 if step > 0 else -1), abs(step))]
        return [((axis, 1), 1), ((axis, 3), 1)] if step == 2 else [(link, 1)]

    needs = {name: len(message["after"]) for name, message in found.items()}
    flying = {unit: [len(names), 0.0] for unit, (_, _, names) in units.items()}
    cores = [set(names) for _, _, names in joined]
    arrivals = [(2 * (low + tiles) * TILE_US, -1, ("own", part)) for part, (_, low, tiles) in PARTS.items()]
    heapq.heapify(arrivals)
    queues, free, steps = {}, {}, []
    clock, ticket = 0.0, 0
    while arrivals or any(queues.values()):
        if arrivals and arrivals[0][0] <= clock:
            what = heapq.heappop(arrivals)[2]
            clock += OP_US
            steps.append(("wait", what))
            for user in users.get(what, []):
                needs[user] -= 1
                if needs[user] == 0:
                    ticket += 1
                    heapq.heappush(queues.setdefault(found[user]["link"], []), (-path(user), ticket, user))
            for names in cores:
                names.discard(what)
            clock += OP_US * sum(1 for names in cores if not names)
            cores = [names for names in cores if names]
            continue
        backlog = {
            link: max(free.get(lane, 0.0) for lane, _ in lanes(link)) for link, queue in queues.items() if queue
        }
        open_links = [(max(until - clock, 0.0), link) for link, until in backlog.items() if until - clock < LEAD_US]
        if open_links:
            _, _, name = heapq.heappop(queues[min(open_links)[1]])
            clock += OP_US
            steps.append(("send", name))
            end = 0.0
            for lane, times in lanes(found[name]["link"]):
                free[lane] = max(clock, free.get(lane, 0.0)) + length[name] * times
                end = max(end, free[lane])
            flight = flying[found[name]["unit"]]
            flight[0] -= 1
            flight[1] = max(flight[1], end + delay[name])
            if flight[0] == 0:
                ticket += 1
                heapq.heappush(arrivals, (flight[1], ticket, found[name]["unit"]))
            continue
        later = [until - LEAD_US + 1e-6 for until in backlog.values()]
        if arrivals:
            later.append(arrivals[0][0])
        clock = max(clock, min(later))
    return steps


def share(found, units, steps):
    at = {step: i for i, step in enumerate(steps)}
    links = {}
    for name, message in found.items():
        if message["part"] is not None:
            links.setdefault(message["link"], []).append((at["send", name], at["wait", message["unit"]]))

    def known(unit, name):
        axis, step = found[name]["link"]
        back = (axis, -step) if axis == "z" else (axis, step)
        over = at["wait", unit]
        return any(sent > over and taken < at["send", name] for sent, taken in links.get(back, []))

    spots, last = {}, []
    rest = [unit for unit in units if unit != OUTER]
    for unit in sorted(rest, key=lambda unit: min(at["send", name] for name in units[unit][2])):
        free = [i for i, old in enumerate(last) if all(known(old, name) for name in units[unit][2])]
        if free:
            spots[unit] = max(free, key=lambda i: at["wait", last[i]])
            last[spots[unit]] = unit
        else:
            spots[unit] = len(last)
            last.append(unit)
    return spots, len(last)


def parity_table(rows, columns):
    i = lax.broadcasted_iota(jnp.int32, (rows, columns), 0)
    j = lax.broadcasted_iota(jnp.int32, (rows, columns), 1)
    both = jnp.bitwise_and(jnp.bitwise_and(i, j), LANES - 1)
    for shift in (4, 2, 1):
        both = jnp.bitwise_xor(both, jnp.right_shift(both, shift))
    return (1 - 2 * jnp.bitwise_and(both, 1)).astype(jnp.bfloat16)


def rotate(tiles, table):
    number, rows, lanes = tiles.shape
    flat = tiles.reshape(number * rows, lanes)
    high = flat.astype(jnp.bfloat16)
    low = (flat - high.astype(jnp.float32)).astype(jnp.bfloat16)
    flat = jnp.dot(jnp.concatenate([high, low], axis=1), table, preferred_element_type=jnp.float32)
    near = 1
    while near < number:
        pairs = flat.reshape(number // (2 * near), 2, near * rows, lanes)
        flat = jnp.concatenate(
            [(pairs[:, 0] + pairs[:, 1])[:, None], (pairs[:, 0] - pairs[:, 1])[:, None]], axis=1
        )
        near *= 2
    return flat.reshape(number, rows, lanes)


def exchange_kernel(
    steps, found, units, joined, spots,
    lw_ref, base_ref, error_ref, momentum_ref, signs_ref, kept_ref,
    whole_ref, fresh_ref, dropped_ref,
    lw, base, error, momentum, signs, kept, part_sums, near, far, mine, outer,
    loads, near_recv, far_recv, outer_recv,
    all_send, message_recv, core_send, core_recv,
):
    rep, shard = lax.axis_index("rep"), lax.axis_index("shard")
    p, c = rep // 2, rep % 2
    x, y_high, z = (shard // 2) % 4, shard % 2, shard // 8
    block = base.shape[2]
    tiles_of_block = block // LANES

    def place_x(bits):
        return {0: x, 1: x + 1 - 2 * (x % 2), 2: (x + 2) % 4, 3: 3 - x}[bits]

    def place_y(bits):
        return (y_high if bits < 2 else 1 - y_high, p if bits % 2 == 0 else 1 - p)

    def place_z(step):
        return (z + step + SIZES["z"]) % SIZES["z"]

    def device(x_bits, y_bits, z_step, core):
        high, low = place_y(y_bits)
        return (low * 2 + core, place_z(z_step) * 8 + place_x(x_bits) * 2 + high)

    other_core = device(0, 0, 0, 1 - c)
    partner = device(0, 1, 0, c)

    def over(link):
        axis, step = link
        return device(step if axis == "x" else 0, step if axis == "y" else 0, step if axis == "z" else 0, c)

    copies = [pltpu.make_async_copy(signs_ref, signs, loads.at[0]), pltpu.make_async_copy(kept_ref, kept, loads.at[1])]
    for slot, b in enumerate((1 - p, p)):
        columns = pl.ds(pl.multiple_of(b * block, block), block)
        copies += [
            pltpu.make_async_copy(lw_ref.at[0, :, columns], lw.at[slot], loads.at[2 + 3 * slot]),
            pltpu.make_async_copy(base_ref.at[:, columns], base.at[slot], loads.at[3 + 3 * slot]),
            pltpu.make_async_copy(error_ref.at[0, :, columns], error.at[slot], loads.at[4 + 3 * slot]),
        ]
    copies.append(pltpu.make_async_copy(momentum_ref, momentum, loads.at[8]))
    for copy in copies[:5]:
        copy.start()

    barrier = pltpu.get_barrier_semaphore()
    peers = [over(link) for link in sorted({message["link"] for message in found.values()})] + [other_core]
    for target in peers:
        pl.semaphore_signal(barrier, inc=1, device_id=target, device_id_type=MESH)

    table = parity_table(2 * LANES, LANES)
    scale = 1.0 / 64.0

    def kept_mask(b):
        places = kept[pl.ds(b, 1), :]
        tile_hot = lax.broadcasted_iota(jnp.int32, (tiles_of_block, places.shape[1]), 0) == jnp.right_shift(places, 7)
        lane_hot = lax.broadcasted_iota(jnp.int32, (LANES, places.shape[1]), 0) == jnp.bitwise_and(places, LANES - 1)
        return lax.dot_general(
            tile_hot.astype(jnp.bfloat16), lane_hot.astype(jnp.bfloat16),
            (((1,), (1,)), ((), ())), preferred_element_type=jnp.float32,
        )[:, None, :]

    def sketch(slot, b, mask):
        for copy in copies[2 + 3 * slot:5 + 3 * slot]:
            copy.wait()
        if slot == 0:
            for copy in copies[5:]:
                copy.start()
        compensated = (base[slot].astype(jnp.float32) - lw[slot].astype(jnp.float32)) + error[slot]
        comp = jnp.stack([compensated[:, t * LANES:(t + 1) * LANES] for t in range(tiles_of_block)])
        rows = pl.ds(pl.multiple_of(b * tiles_of_block, tiles_of_block), tiles_of_block)
        turn = signs[rows, :].astype(jnp.float32)[:, None, :]
        rotated = rotate(comp * turn, table) * scale
        back = rotate(jnp.where(mask > 0.5, rotated, 0.0), table) * (turn * scale)
        half = tiles_of_block // 2
        for t in range(tiles_of_block):
            part_sums[2 * b + t // half, :, pl.ds((t % half) * LANES, LANES)] = back[t]
        return comp - back

    def keep_rest(b, rest):
        for t in range(tiles_of_block):
            dropped_ref[:, pl.ds(pl.multiple_of(b * block + t * LANES, LANES), LANES)] = rest[t]

    def remote(source, target, send, recv, where):
        return pltpu.make_async_remote_copy(
            src_ref=source, dst_ref=target, send_sem=send, recv_sem=recv, device_id=where, device_id_type=MESH
        )

    def at(region, tiles):
        def span(axis):
            i, cuts = region[axis]
            wide = SIZES[axis] // cuts
            return pl.ds(i * wide, wide)

        spot_x = span("x") if isinstance(region["x"], tuple) else place_x(region["x"])
        spot_z = span("z") if isinstance(region["z"], tuple) else place_z(region["z"])
        if isinstance(region["y"], tuple):
            high, low = pl.ds(region["y"][0], 2 // region["y"][1]), slice(None)
        else:
            high, low = place_y(region["y"])
        return whole_ref.at[spot_z, spot_x, high, low, c, :, pl.ds(tiles[0] * LANES, (tiles[1] - tiles[0]) * LANES)]

    first = next(iter(PARTS.values()))[2] * LANES
    to_far = []
    for i, columns in enumerate((pl.ds(0, first), pl.ds(first, QUARTER - first))):
        to_far.append(remote(
            part_sums.at[2 * (1 - p) + 1 - c, :, columns], near.at[0, :, columns], all_send, near_recv.at[i], other_core
        ))
    to_mine = remote(part_sums.at[2 * p + 1 - c], near.at[1], all_send, near_recv.at[2], other_core)
    copies[0].wait()
    copies[1].wait()
    first_mask = kept_mask(1 - p)
    rest = sketch(0, 1 - p, first_mask)
    pl.semaphore_wait(barrier, len(peers))
    for copy in to_far:
        copy.start()
    keep_rest(1 - p, rest)
    rest = sketch(1, p, kept_mask(p))
    to_mine.start()
    pieces = {}
    for i, (part, (_, low, tiles)) in enumerate(PARTS.items()):
        columns = pl.ds(low * LANES, tiles * LANES)
        if i < 2:
            to_far[i].wait_recv()
        mine[:, columns] = part_sums[2 * (1 - p) + c, :, columns] + near[0, :, columns]
        pieces[part] = remote(mine.at[:, columns], far.at[:, columns], all_send, far_recv.at[i], partner)
        pieces[part].start()
    keep_rest(p, rest)
    to_mine.wait_recv()
    copies[8].wait()

    mine_outer, their_outer = outer.at[2 * p + c], outer.at[2 * (1 - p) + c]
    outer_far = remote(mine_outer, mine_outer, all_send, outer_recv.at[0], partner)
    outer_near = remote(mine_outer, mine_outer, all_send, outer_recv.at[1], other_core)
    outer_last = remote(their_outer, their_outer, all_send, outer_recv.at[2], other_core)

    def send(name):
        message = found[name]
        axis, step = message["link"]
        region = dict(message["region"])
        region[axis] = region[axis] + step if axis == "z" else region[axis] ^ step
        place = at(region, message["tiles"])
        remote(
            place, place, all_send, message_recv.at[spots[message["unit"]]], over(message["link"]),
        ).start()

    def take(unit):
        region, tiles, _ = units[unit]
        place = at(region, tiles)
        remote(place, place, core_send, message_recv.at[spots[unit]], other_core).wait_recv()

    def own(part):
        _, low, tiles = PARTS[part]
        columns = pl.ds(low * LANES, tiles * LANES)
        pieces[part].wait_recv()
        total = (part_sums[2 * p + c, :, columns] + near[1, :, columns]) + far[:, columns]
        step = total * 0.25
        outer[2 * p + c, :, columns] = step
        wide = pl.ds(pl.multiple_of((2 * p + c) * QUARTER + low * LANES, LANES), tiles * LANES)
        fresh = 0.9 * momentum[:, wide] + step
        held = pl.ds(pl.multiple_of(c * QUARTER + low * LANES, LANES), tiles * LANES)
        lowered = base[1, :, held].astype(jnp.float32) - 0.7 * (step + 0.9 * fresh)
        whole_ref[z, x, y_high, p, c, :, columns] = lowered.astype(jnp.bfloat16)

    def finish():
        from_core = outer.at[2 * p + 1 - c]
        remote(from_core, from_core, all_send, outer_recv.at[1], other_core).wait_recv()
        from_core = outer.at[2 * (1 - p) + 1 - c]
        remote(from_core, from_core, all_send, outer_recv.at[2], other_core).wait_recv()
        for q in range(4):
            columns = pl.ds(q * QUARTER, QUARTER)
            fresh_ref[:, columns] = 0.9 * momentum[:, columns] + outer[q]

    waiting = [(set(group), region, tiles) for region, tiles, group in joined]
    outer_at = steps.index(("wait", OUTER))
    for i, (kind, what) in enumerate(steps):
        if i == outer_at + FINISH_AFTER:
            finish()
        if kind == "send":
            if what == OUTER:
                outer_far.start()
                outer_near.start()
            else:
                send(what)
            continue
        if what == OUTER:
            remote(their_outer, their_outer, all_send, outer_recv.at[0], partner).wait_recv()
            outer_last.start()
            continue
        if what[0] == "own":
            own(what[1])
        else:
            take(what)
        for group, _, _ in waiting:
            group.discard(what)
        for _, region, tiles in [entry for entry in waiting if not entry[0]]:
            place = at(region, tiles)
            remote(place, place, core_send, core_recv, other_core).start()
        waiting = [entry for entry in waiting if entry[0]]
    if outer_at + FINISH_AFTER >= len(steps):
        finish()

    for part, (order, low, tiles) in PARTS.items():
        columns = pl.ds(low * LANES, tiles * LANES)
        for stage in (1, 2, 3):
            ends = {axis: 1 for axis in AXES}
            for axis in order[:stage - 1]:
                ends[axis] = SIZES[axis]
            ends[order[stage - 1]] = SIZES[order[stage - 1]] - 1
            for high, low_y in {1: [(1, 1)], 3: [(1, 2), (1, 1)], 4: [(2, 2)]}[ends["y"]]:
                place = whole_ref.at[
                    pl.ds(0, ends["z"]), pl.ds(0, ends["x"]), pl.ds(0, high), pl.ds(0, low_y), c, :, columns
                ]
                remote(place, place, all_send, core_recv, other_core).wait_send()
    for copy in to_far + [to_mine] + list(pieces.values()) + [outer_far, outer_near, outer_last]:
        copy.wait_send()
    everything = whole_ref.at[:, :, :, :, c]
    remote(everything, everything, core_send, core_recv, other_core).wait_send()
    everything = whole_ref.at[:, :, :, :, 1 - c]
    remote(everything, everything, core_send, core_recv, other_core).wait_recv()


def store_kernel(whole_ref, fresh_ref, dropped_ref, base_out, error_out, momentum_out, sems):
    copies = [
        pltpu.make_async_copy(fresh_ref, momentum_out, sems.at[0]),
        pltpu.make_async_copy(dropped_ref, error_out.at[0], sems.at[1]),
    ]
    for z in range(whole_ref.shape[0]):
        for low in range(2):
            for core in range(2):
                copies.append(pltpu.make_async_copy(
                    whole_ref.at[z, :, :, low, core],
                    base_out.at[z, :, :, :, pl.ds((2 * low + core) * QUARTER, QUARTER)],
                    sems.at[len(copies)],
                ))
    for copy in copies:
        copy.start()
    for copy in copies:
        copy.wait()


def shards(local_weights, base, error, momentum, signs, kept):
    rows, width = base.shape
    vmem = pl.BlockSpec(memory_space=pltpu.VMEM)
    hbm = pl.BlockSpec(memory_space=pl.ANY)
    held = lambda array: pltpu.with_memory_space_constraint(array, pltpu.VMEM)
    stay = lambda array: pltpu.with_memory_space_constraint(array, pltpu.HBM)
    found, units = messages()
    joined = forwards(found)
    steps = schedule(found, units, joined)
    spots, number = share(found, units, steps)
    dma = pltpu.SemaphoreType.DMA
    whole, fresh, dropped = pl.pallas_call(
        functools.partial(exchange_kernel, steps, found, units, joined, spots),
        out_shape=(
            pltpu.VMEM((8, 4, 2, 2, 2, rows, QUARTER), jnp.bfloat16),
            pltpu.VMEM((rows, width), jnp.float32),
            pltpu.VMEM((rows, width), jnp.float32),
        ),
        in_specs=[hbm] * 6,
        out_specs=(vmem, vmem, vmem),
        scratch_shapes=[
            pltpu.VMEM((2, rows, width // 2), jnp.bfloat16),
            pltpu.VMEM((2, rows, width // 2), jnp.bfloat16),
            pltpu.VMEM((2, rows, width // 2), jnp.float32),
            pltpu.VMEM((rows, width), jnp.float32),
            pltpu.VMEM((width // LANES, LANES), jnp.int32),
            pltpu.VMEM(kept.shape, jnp.int32),
            pltpu.VMEM((4, rows, QUARTER), jnp.float32),
            pltpu.VMEM((2, rows, QUARTER), jnp.float32),
            pltpu.VMEM((rows, QUARTER), jnp.float32),
            pltpu.VMEM((rows, QUARTER), jnp.float32),
            pltpu.VMEM((4, rows, QUARTER), jnp.float32),
            dma((9,)), dma((3,)), dma((3,)), dma((3,)), dma, dma((number,)), dma, dma,
        ],
        compiler_params=pltpu.CompilerParams(
            collective_id=0, has_side_effects=True, vmem_limit_bytes=16 << 20
        ),
        name="exchange",
    )(
        stay(local_weights), stay(base), stay(error), stay(momentum),
        stay(signs.reshape(width // LANES, LANES)), stay(kept),
    )

    new_base, new_error, new_momentum = pl.pallas_call(
        store_kernel,
        out_shape=(
            jax.ShapeDtypeStruct((8, 4, 2, rows, width), jnp.bfloat16),
            jax.ShapeDtypeStruct((1, rows, width), jnp.float32),
            jax.ShapeDtypeStruct((rows, width), jnp.float32),
        ),
        in_specs=[vmem] * 3,
        out_specs=(hbm, hbm, hbm),
        scratch_shapes=[dma((34,))],
        compiler_params=pltpu.CompilerParams(vmem_limit_bytes=16 << 20),
        name="store",
    )(held(whole), held(fresh), held(dropped))
    return (new_base.reshape(64 * rows, width), new_error, new_momentum)


def solution(mesh):
    in_specs = (
        P("rep", "shard", None),
        P("shard", None),
        P("rep", "shard", None),
        P("shard", None),
        P(),
        P(),
    )
    out_specs = (P(), P("rep", "shard", None), P("shard", None))
    return jax.shard_map(shards, mesh=mesh, in_specs=in_specs, out_specs=out_specs, check_vma=False)
```
